128 devices in a mesh: rows: 128 (over x, y, z, core).
Axes of the slice: x: 4, y: 4, z: 4, core: 2. Of those that a mesh axis runs over, the one named last changes fastest.
Arguments:
- features: bfloat16 [524288, 128], P('rows'), may hold values from -6 to 6
- weight: bfloat16 [128, 256], replicated, may hold values from -0.5 to 0.5
- adjacency_tiles: bfloat16 [4096, 6, 128, 128], P('rows'), may hold values from -0.15625 to 0.15625
- tile_columns: int32 [4096, 6], P('rows'), may hold values from 0 to 159
- send_rows: int32 [128, 128, 128], P('rows'), may hold values from -1 to 4095, as said below
- hub_owner: int32 [4], replicated, may hold values from 0 to 127
- hub_rows: int32 [4, 128], replicated, may hold values from 0 to 4095
- hub_tiles: bfloat16 [4, 524288, 128], P(None, 'rows'), may hold values from -0.15625 to 0.15625
- cotangent: bfloat16 [524288, 256], P('rows'), may hold values from -6 to 6
Outputs:
- output: bfloat16 [524288, 256], P('rows')
- grad_features: bfloat16 [524288, 128], P('rows')
- grad_weight: float32 [128, 256], replicated
The draws below stay inside these ranges and needn't reach their ends.
Inputs may be any that keep to these rules, and one draw needn't show every extreme that they name: `send_rows`: in each list the live entries (not -1) come first; every list has 32 or more live entries, and every device has one full list of 128 live entries to some peer. Rows may repeat.
All inputs are finite; a program needn't handle non-finite values.
Results may differ from the reference program's by a relative error of at most 0.0075.
Values may be sent and summed in bfloat16 or wider, within the bound.
No kernel may reach another device: no remote copies, remote signals or barrier semaphores. Data moves between devices by JAX's collectives and lax.ppermute only.
A program may use at most 192 MiB of HBM per device.

```python
import jax
import jax.numpy as jnp
from jax import lax

F = 128
H = 256
BLK = 128
ROWS_DEV = 4096
TPR = 6
SECTIONS = 4
NODES = 524288
N_ROWS = 128


def draw_send_rows(key, part):
    key = jax.random.fold_in(key, 7)
    key_rows, key_fill, key_full = jax.random.split(key, 3)
    chosen = jax.random.randint(key_rows, (N_ROWS, N_ROWS, BLK), 0, ROWS_DEV)
    filled = jax.random.randint(key_fill, (N_ROWS, N_ROWS), BLK // 4, BLK + 1)
    offset = jax.random.randint(key_full, (N_ROWS,), 1, N_ROWS)
    source = jnp.arange(N_ROWS)[:, None]
    target = jnp.arange(N_ROWS)[None, :]
    filled = jnp.where(target == (source + offset[:, None]) % N_ROWS, BLK, filled)
    live_slot = jnp.arange(BLK)[None, None, :] < filled[:, :, None]
    return jnp.where(live_slot, chosen, -1).astype(jnp.int32)


def touch_ends(array, rng, least, high):
    spot = [jax.random.randint(jax.random.fold_in(rng, axis), (), 0, length) for axis, length in enumerate(array.shape)]
    longest = array.shape.index(max(array.shape))
    neighbour = spot[:longest] + [(spot[longest] + 1) % array.shape[longest]] + spot[longest + 1:]
    return array.at[tuple(spot)].set(least).at[tuple(neighbour)].set(high)


def block_levels(rng, dims, shards, low, high):
    level = 1.0
    for axis_at, blocks in shards:
        steps = jax.random.uniform(jax.random.fold_in(jax.random.fold_in(rng, 6), axis_at), (blocks,), jnp.float32, low / len(shards), high / len(shards))
        level = level * jnp.repeat(jnp.exp(steps), dims[axis_at] // blocks).reshape((-1,) + (1,) * (len(dims) - 1 - axis_at))
    return level


def centred(own_key, shape, deviation, most, cuts=(), kind=jnp.bfloat16):
    entries = deviation * jax.random.normal(own_key, shape, jnp.float32)
    if cuts:
        entries = entries * block_levels(own_key, shape, cuts, -0.22, 0.18)
    return jnp.clip(entries, -most, most).astype(kind)


def setup_inputs(seed: int = 0) -> dict:
    key_list = jax.random.split(jax.random.key(seed), 10)
    features = centred(key_list[0], (NODES, F), 1.0, 6.0, ((0, 128),))
    weight = centred(key_list[1], (F, H), F ** -0.5, 0.5)
    adjacency_tiles = centred(key_list[2], (NODES // BLK, TPR, BLK, BLK), (TPR * BLK + SECTIONS * BLK) ** -0.5, 0.15625, ((0, 128),))
    tile_columns = touch_ends(jax.random.randint(key_list[3], (NODES // BLK, TPR), 0, ROWS_DEV // BLK + N_ROWS), jax.random.fold_in(key_list[3], 1), 0, (ROWS_DEV // BLK + N_ROWS) - 1).astype(jnp.int32)
    send_rows = draw_send_rows(jax.random.fold_in(key_list[9], 71), 0)
    hub_owner = touch_ends(jax.random.randint(key_list[5], (SECTIONS,), 0, N_ROWS), jax.random.fold_in(key_list[5], 1), 0, N_ROWS - 1).astype(jnp.int32)
    hub_rows = touch_ends(jax.random.randint(key_list[6], (SECTIONS, BLK), 0, ROWS_DEV), jax.random.fold_in(key_list[6], 1), 0, ROWS_DEV - 1).astype(jnp.int32)
    hub_tiles = centred(key_list[7], (SECTIONS, NODES, BLK), (TPR * BLK + SECTIONS * BLK) ** -0.5, 0.15625, ((1, 128),))
    cotangent = centred(key_list[8], (NODES, H), 1.0, 6.0, ((0, 128),))
    return {"features": features, "weight": weight, "adjacency_tiles": adjacency_tiles, "tile_columns": tile_columns, "send_rows": send_rows, "hub_owner": hub_owner, "hub_rows": hub_rows, "hub_tiles": hub_tiles, "cotangent": cotangent}


def reference(features, weight, adjacency_tiles, tile_columns, send_rows, hub_owner, hub_rows, hub_tiles, cotangent):
    blocks = ROWS_DEV // BLK
    peers = N_ROWS
    projected = jnp.dot(features, weight, preferred_element_type=jnp.float32).astype(jnp.bfloat16)
    proj_dev = projected.reshape(peers, ROWS_DEV, H)
    tiles_dev = adjacency_tiles.reshape(peers, blocks, TPR, BLK, BLK)
    columns_dev = tile_columns.reshape(peers, blocks, TPR)
    source_ids = jnp.arange(peers, dtype=jnp.int32)[:, None]

    def halo_for(device):
        lists = send_rows[:, device, :]
        live_slot = lists >= 0
        safe_rows = jnp.maximum(lists, 0).astype(jnp.int32)
        return (live_slot, safe_rows)

    def forward_dev(device):
        live_slot, safe_rows = halo_for(device)
        halo = jnp.where(live_slot[:, :, None], proj_dev[source_ids, safe_rows], jnp.zeros((), jnp.bfloat16))
        own_blocks = proj_dev[device].reshape(blocks, BLK, H)
        columns = jnp.concatenate([own_blocks, halo], axis=0)
        gathered = columns[columns_dev[device]]
        tiled = jnp.einsum('btij,btjh->bih', tiles_dev[device].astype(jnp.float32), gathered.astype(jnp.float32))
        return tiled.reshape(ROWS_DEV, H)
    tiled_all = lax.map(forward_dev, jnp.arange(peers, dtype=jnp.int32)).reshape(ROWS_DEV * peers, H)
    preact = tiled_all
    for section in range(SECTIONS):
        hub_block = proj_dev[hub_owner[section], hub_rows[section]]
        preact = preact + jnp.dot(hub_tiles[section], hub_block, preferred_element_type=jnp.float32)
    output = jax.nn.gelu(preact).astype(jnp.bfloat16)
    activated, pullback = jax.vjp(jax.nn.gelu, preact)
    grad_preact = pullback(cotangent.astype(jnp.float32))[0].astype(jnp.bfloat16)
    grad_dev = grad_preact.reshape(peers, ROWS_DEV, H)

    def backward_dev(accumulated, device):
        live_slot, safe_rows = halo_for(device)
        grad_blocks = grad_dev[device].reshape(blocks, BLK, H).astype(jnp.float32)
        contribution = jnp.einsum('btij,bih->btjh', tiles_dev[device].astype(jnp.float32), grad_blocks)
        summed = jax.ops.segment_sum(contribution.reshape(blocks * TPR, BLK, H), columns_dev[device].reshape(-1), blocks + peers)
        accumulated = accumulated.at[device].add(summed[:blocks].reshape(ROWS_DEV, H))
        halo_rounded = lax.optimization_barrier(summed[blocks:].astype(jnp.bfloat16)).astype(jnp.float32)
        halo_part = jnp.where(live_slot[:, :, None], halo_rounded, jnp.zeros((), jnp.float32))
        accumulated = accumulated.at[source_ids, safe_rows].add(halo_part)
        return (accumulated, None)
    accumulated, unused = lax.scan(backward_dev, jnp.zeros((peers, ROWS_DEV, H), jnp.float32), jnp.arange(peers, dtype=jnp.int32))
    for section in range(SECTIONS):
        hub_sum = jnp.dot(hub_tiles[section].T, grad_preact, preferred_element_type=jnp.float32)
        accumulated = accumulated.at[hub_owner[section], hub_rows[section]].add(hub_sum)
    grad_proj = accumulated.reshape(ROWS_DEV * peers, H).astype(jnp.bfloat16)
    grad_features = jnp.dot(grad_proj, weight.T, preferred_element_type=jnp.float32).astype(jnp.bfloat16)
    grad_weight = jnp.dot(features.T, grad_proj, preferred_element_type=jnp.float32)
    return (output, grad_features, grad_weight)
```

```python
import functools

import jax
import jax.numpy as jnp
from jax import lax
from jax.experimental import pallas as pl
from jax.experimental.pallas import tpu as pltpu
from jax.sharding import PartitionSpec as P

BF = jnp.bfloat16
F32 = jnp.float32
VMEM_LIMIT = 56 * 2**20
UNROLL = 32
PAD = 8
GELU_A = 0.7978845608028654
GELU_B = 0.044715


def hub_gather_kernel(rows_ref, x_ref, out_ref, wide):
    peers, sections, width = out_ref.shape
    wide[...] = x_ref[...].astype(F32)
    group = 16

    def body(step, carry):
        first = step * group
        for section in range(sections):
            for slot in range(group):
                row = rows_ref[section * peers + first + slot]
                out_ref[first + slot, section : section + 1, :] = wide[pl.ds(row, 1), :]
        return carry

    lax.fori_loop(0, peers // group, body, 0)


def hub_gather(features, hub_rows):
    sections, peers = hub_rows.shape
    rows, width = features.shape
    return pl.pallas_call(
        hub_gather_kernel,
        grid_spec=pltpu.PrefetchScalarGridSpec(
            num_scalar_prefetch=1,
            grid=(1,),
            in_specs=[pl.BlockSpec((rows, width), lambda i, *_: (0, 0))],
            out_specs=pl.BlockSpec((peers, sections, width), lambda i, *_: (0, 0, 0)),
            scratch_shapes=[pltpu.VMEM((rows, width), F32)],
        ),
        out_shape=jax.ShapeDtypeStruct((peers, sections, width), F32),
        compiler_params=pltpu.CompilerParams(vmem_limit_bytes=VMEM_LIMIT),
    )(hub_rows.reshape(-1), features)


def live_groups(list_ref, start, slots, group):
    count = jnp.int32(0)
    for first in range(0, slots, group):
        count = count + (list_ref[start + first] >= 0).astype(jnp.int32)
    return count


def gather_kernel(lists, list_ref, x_ref, out_ref, wide, buffer):
    step = pl.program_id(0)
    rows = x_ref.shape[0]
    slots = buffer.shape[0]

    @pl.when(step == 0)
    def _():
        wide[pl.ds(0, PAD), :] = jnp.zeros((PAD, wide.shape[1]), F32)
        wide[pl.ds(PAD, rows), :] = x_ref[...].astype(F32)

    for k in range(lists):
        start = (step * lists + k) * slots
        buffer[...] = jnp.zeros_like(buffer)

        def body(group, carry):
            base = pl.multiple_of(group * UNROLL, UNROLL)
            for slot in range(UNROLL):
                row = list_ref[start + base + slot]
                buffer[pl.ds(base + slot, 1), :] = wide[pl.ds(row + PAD, 1), :]
            return carry

        lax.fori_loop(0, live_groups(list_ref, start, slots, UNROLL), body, 0)
        out_ref[k] = buffer[...].astype(BF)


def gather_rows(features, send_lists):
    peers, slots = send_lists.shape
    rows, width = features.shape
    lists = 8
    return pl.pallas_call(
        functools.partial(gather_kernel, lists),
        grid_spec=pltpu.PrefetchScalarGridSpec(
            num_scalar_prefetch=1,
            grid=(peers // lists,),
            in_specs=[pl.BlockSpec((rows, width), lambda i, *_: (0, 0))],
            out_specs=pl.BlockSpec((lists, slots, width), lambda i, *_: (i, 0, 0)),
            scratch_shapes=[
                pltpu.VMEM((rows + PAD, width), F32),
                pltpu.VMEM((slots, width), F32),
            ],
        ),
        out_shape=jax.ShapeDtypeStruct((peers, slots, width), BF),
        compiler_params=pltpu.CompilerParams(vmem_limit_bytes=VMEM_LIMIT),
    )(send_lists.reshape(-1), features)


def layer_kernel(
    group,
    columns_ref,
    x_hbm,
    halo_hbm,
    hub_ref,
    w_ref,
    tiles_ref,
    hub_tiles_ref,
    cot_ref,
    out_ref,
    send_ref,
    own_ref,
    features,
    adjoint,
    hub_adjoint,
    grad_w,
    extra,
    sems,
):
    step = pl.program_id(0)
    steps = pl.num_programs(0)
    per_block = tiles_ref.shape[1]
    blk = tiles_ref.shape[2]
    own_blocks = x_hbm.shape[0]
    peers = halo_hbm.shape[0]
    sections = hub_tiles_ref.shape[0]
    width = hub_ref.shape[1]

    @pl.when(step == 0)
    def _():
        own = pltpu.make_async_copy(x_hbm, features.at[pl.ds(0, own_blocks)], sems.at[0])
        halo = pltpu.make_async_copy(halo_hbm, features.at[pl.ds(own_blocks, peers)], sems.at[1])
        own.start()
        halo.start()

        def clear(block, carry):
            adjoint[block] = jnp.zeros((width, blk), F32)
            return carry

        lax.fori_loop(0, own_blocks + peers, clear, 0, unroll=4)
        hub_adjoint[...] = jnp.zeros_like(hub_adjoint)
        grad_w[...] = jnp.zeros_like(grad_w)
        own.wait()
        halo.wait()

    weight = w_ref[...]
    weight_twice = jnp.concatenate([weight, weight], axis=0)
    hub_slab = jnp.concatenate([hub_tiles_ref[s] for s in range(sections)], axis=1)
    hub_part = jnp.dot(hub_slab, hub_ref[...], preferred_element_type=F32)
    projected_back = []
    for u in range(group):
        places = [columns_ref[(step * group + u) * per_block + t] for t in range(per_block)]
        slab = jnp.concatenate([tiles_ref[u, t] for t in range(per_block)], axis=1)
        blocks = jnp.concatenate([features[place] for place in places], axis=0)
        rows = pl.ds(u * blk, blk)
        z = jnp.dot(slab, blocks, preferred_element_type=F32) + hub_part[u * blk : (u + 1) * blk]
        z_high = z.astype(BF)
        z_low = (z - z_high.astype(F32)).astype(BF)
        preact = jnp.dot(
            jnp.concatenate([z_high, z_low], axis=1), weight_twice, preferred_element_type=F32
        )
        square = preact * preact
        t = jnp.tanh(preact * (GELU_A + (GELU_A * GELU_B) * square))
        half = 0.5 * (1.0 + t)
        out_ref[rows, :] = (preact * half).astype(BF)
        slope = half + (0.5 * preact) * (1.0 - t * t) * (GELU_A + (3.0 * GELU_A * GELU_B) * square)
        grad = (cot_ref[rows, :].astype(F32) * slope).astype(BF)
        grad_w[...] += lax.dot_general(
            z_high, grad, (((0,), (0,)), ((), ())), preferred_element_type=F32
        )
        back = lax.dot_general(
            weight, grad, (((1,), (1,)), ((), ())), preferred_element_type=F32
        ).astype(BF)
        projected_back.append(back)
        spread = jnp.dot(back, slab, preferred_element_type=F32)
        for t in range(per_block):
            adjoint[places[t]] += spread[:, t * blk : (t + 1) * blk]
    hub_adjoint[...] += jnp.dot(
        jnp.concatenate(projected_back, axis=1), hub_slab, preferred_element_type=F32
    )

    @pl.when(step == steps - 1)
    def _():
        for s in range(sections):
            extra[:, s, :] = hub_adjoint[:, s * blk : (s + 1) * blk].T
        total = grad_w[...]
        high = total.astype(BF).astype(F32)
        low = total - high
        pieces = total.shape[1] // width
        for piece in range(pieces):
            part = slice(piece * width, (piece + 1) * width)
            extra[:, sections + piece, :] = high[:, part]
            extra[:, sections + pieces + piece, :] = low[:, part]

        def finish_own(block, carry):
            own_ref[pl.ds(pl.multiple_of(block * blk, blk), blk), :] = adjoint[block].T
            return carry

        lax.fori_loop(0, own_blocks, finish_own, 0, unroll=4)

        def finish_halo(peer, carry):
            turned = adjoint[own_blocks + peer].T
            send_ref[peer] = jnp.concatenate([turned, extra[peer]], axis=0).astype(BF)
            return carry

        lax.fori_loop(0, peers, finish_halo, 0, unroll=4)


def layer(features, halo, hub, weight, tiles, tile_columns, hub_tiles, cotangent):
    blocks, per_block, blk, _ = tiles.shape
    peers = halo.shape[0]
    width, width_out = weight.shape
    sections = hub_tiles.shape[0]
    rows = blocks * blk
    group = 4
    extras = sections + 2 * (width_out // width)
    return pl.pallas_call(
        functools.partial(layer_kernel, group),
        grid_spec=pltpu.PrefetchScalarGridSpec(
            num_scalar_prefetch=1,
            grid=(blocks // group,),
            in_specs=[
                pl.BlockSpec(memory_space=pl.ANY),
                pl.BlockSpec(memory_space=pl.ANY),
                pl.BlockSpec((sections * blk, width), lambda i, *_: (0, 0)),
                pl.BlockSpec((width, width_out), lambda i, *_: (0, 0)),
                pl.BlockSpec((group, per_block, blk, blk), lambda i, *_: (i, 0, 0, 0)),
                pl.BlockSpec((sections, group * blk, blk), lambda i, *_: (0, i, 0)),
                pl.BlockSpec((group * blk, width_out), lambda i, *_: (i, 0)),
            ],
            out_specs=[
                pl.BlockSpec((group * blk, width_out), lambda i, *_: (i, 0)),
                pl.BlockSpec((peers, blk + extras, width), lambda i, *_: (0, 0, 0)),
                pl.BlockSpec((rows, width), lambda i, *_: (0, 0)),
            ],
            scratch_shapes=[
                pltpu.VMEM((blocks + peers, blk, width), BF),
                pltpu.VMEM((blocks + peers, width, blk), F32),
                pltpu.VMEM((width, sections * blk), F32),
                pltpu.VMEM((width, width_out), F32),
                pltpu.VMEM((peers, extras, width), F32),
                pltpu.SemaphoreType.DMA((2,)),
            ],
        ),
        out_shape=[
            jax.ShapeDtypeStruct((rows, width_out), BF),
            jax.ShapeDtypeStruct((peers, blk + extras, width), BF),
            jax.ShapeDtypeStruct((rows, width), F32),
        ],
        compiler_params=pltpu.CompilerParams(vmem_limit_bytes=VMEM_LIMIT),
    )(
        tile_columns.reshape(-1),
        features.reshape(blocks, blk, width),
        halo,
        hub,
        weight,
        tiles,
        hub_tiles,
        cotangent,
    )


def scatter_kernel(lists, list_ref, back_ref, own_ref, out_ref, t0, t1, t2, t3, buffer):
    step = pl.program_id(0)
    steps = pl.num_programs(0)
    totals = (t0, t1, t2, t3)
    slots = buffer.shape[0]
    rows = own_ref.shape[0]

    @pl.when(step == 0)
    def _():
        for total in totals:
            total[...] = jnp.zeros_like(total)

    for k in range(lists):
        start = (step * lists + k) * slots
        buffer[...] = back_ref[k, :slots, :].astype(F32)

        def body(group, carry):
            base = pl.multiple_of(group * UNROLL, UNROLL)
            for slot in range(0, UNROLL, 4):
                places = [list_ref[start + base + slot + v] + PAD for v in range(4)]
                sums = [
                    totals[v][pl.ds(places[v], 1), :] + buffer[pl.ds(base + slot + v, 1), :]
                    for v in range(4)
                ]
                for v in range(4):
                    totals[v][pl.ds(places[v], 1), :] = sums[v]
            return carry

        lax.fori_loop(0, live_groups(list_ref, start, slots, UNROLL), body, 0)

    @pl.when(step == steps - 1)
    def _():
        live = pl.ds(PAD, rows)
        out_ref[...] = ((t0[live, :] + t1[live, :]) + (t2[live, :] + t3[live, :])) + own_ref[...]


def scatter_rows(send_lists, returned, own):
    peers, slots = send_lists.shape
    rows, width = own.shape
    lists = 8
    return pl.pallas_call(
        functools.partial(scatter_kernel, lists),
        grid_spec=pltpu.PrefetchScalarGridSpec(
            num_scalar_prefetch=1,
            grid=(peers // lists,),
            in_specs=[
                pl.BlockSpec((lists, returned.shape[1], width), lambda i, *_: (i, 0, 0)),
                pl.BlockSpec((rows, width), lambda i, *_: (0, 0)),
            ],
            out_specs=pl.BlockSpec((rows, width), lambda i, *_: (0, 0)),
            scratch_shapes=[pltpu.VMEM((rows + PAD, width), F32)] * 4
            + [pltpu.VMEM((slots, width), F32)],
        ),
        out_shape=jax.ShapeDtypeStruct((rows, width), F32),
        compiler_params=pltpu.CompilerParams(vmem_limit_bytes=VMEM_LIMIT),
    )(send_lists.reshape(-1), returned, own)


def finish_kernel(owned_ref, rows_ref, hub_ref, total_ref, out_ref, total):
    sections, peers, _ = hub_ref.shape
    total[...] = total_ref[...]
    group = 16
    for section in range(sections):

        @pl.when(owned_ref[section] != 0)
        def _():
            def body(step, carry):
                first = pl.multiple_of(step * group, group)
                for slot in range(group):
                    row = rows_ref[section * peers + first + slot]
                    total[pl.ds(row, 1), :] += hub_ref[section, pl.ds(first + slot, 1), :]
                return carry

            lax.fori_loop(0, peers // group, body, 0)

    out_ref[...] = total[...].astype(BF)


def finish(total, hub_sums, hub_rows, owned):
    rows, width = total.shape
    sections, peers, _ = hub_sums.shape
    return pl.pallas_call(
        finish_kernel,
        grid_spec=pltpu.PrefetchScalarGridSpec(
            num_scalar_prefetch=2,
            grid=(1,),
            in_specs=[
                pl.BlockSpec((sections, peers, width), lambda i, *_: (0, 0, 0)),
                pl.BlockSpec((rows, width), lambda i, *_: (0, 0)),
            ],
            out_specs=pl.BlockSpec((rows, width), lambda i, *_: (0, 0)),
            scratch_shapes=[pltpu.VMEM((rows, width), F32)],
        ),
        out_shape=jax.ShapeDtypeStruct((rows, width), BF),
        compiler_params=pltpu.CompilerParams(vmem_limit_bytes=VMEM_LIMIT),
    )(owned.astype(jnp.int32), hub_rows.reshape(-1), hub_sums, total)


def exchange(array):
    return lax.all_to_all(array, "rows", split_axis=0, concat_axis=0, tiled=True)


def body(
    features,
    weight,
    adjacency_tiles,
    tile_columns,
    send_rows,
    hub_owner,
    hub_rows,
    hub_tiles,
    cotangent,
):
    device = lax.axis_index("rows")
    sections, peers = hub_rows.shape
    width, width_out = weight.shape
    pieces = width_out // width
    send_lists = send_rows[0]

    hub_out = hub_gather(features, hub_rows).astype(BF)
    hub_in = exchange(hub_out)
    hub_mine = hub_in[hub_owner, jnp.arange(sections)]
    hub_all = lax.all_gather(hub_mine, "rows")
    hub = hub_all.transpose(1, 0, 2).reshape(sections * peers, width)

    outgoing = gather_rows(features, send_lists)
    halo = exchange(outgoing)
    output, adjoint, own = layer(
        features, halo, hub, weight, adjacency_tiles, tile_columns, hub_tiles, cotangent
    )
    returned = exchange(adjoint)

    blk = send_lists.shape[1]
    sums = jnp.sum(returned[:, blk:, :].astype(F32), axis=0)
    weight_row = sums[sections : sections + pieces] + sums[sections + pieces :]
    high = weight_row.astype(BF)
    low = (weight_row - high.astype(F32)).astype(BF)
    mine = jnp.concatenate([sums[:sections].astype(BF), high, low], axis=0)
    everyone = exchange(jnp.broadcast_to(mine[None], (peers,) + mine.shape)).astype(F32)

    total = scatter_rows(send_lists, returned, own)
    hub_sums = everyone[:, :sections].transpose(1, 0, 2)
    grad_weight = everyone[:, sections : sections + pieces] + everyone[:, sections + pieces :]
    grad_features = finish(total, hub_sums, hub_rows, hub_owner == device)
    return (output, grad_features, grad_weight.reshape(width, width_out))


def solution(mesh):
    return jax.shard_map(
        body,
        mesh=mesh,
        in_specs=(
            P("rows", None),
            P(),
            P("rows", None, None, None),
            P("rows", None),
            P("rows", None, None),
            P(),
            P(),
            P(None, "rows", None),
            P("rows", None),
        ),
        out_specs=(P("rows", None), P("rows", None), P()),
        check_vma=False,
    )
```

```python
import functools

import jax
import jax.numpy as jnp
from jax import lax
from jax.experimental import pallas as pl
from jax.experimental.pallas import tpu as pltpu
from jax.sharding import PartitionSpec as P

BF = jnp.bfloat16
F32 = jnp.float32
MIB = 2**20
UNROLL = 32
PAD = 8
GELU_A = 0.7978845608028654
GELU_B = 0.044715


def live_groups(list_ref, start, slots, group):
    count = jnp.int32(0)
    for first in range(0, slots, group):
        count = count + (list_ref[start + first] >= 0).astype(jnp.int32)
    return count


def gather_kernel(lists, slots, list_ref, hub_ref, x_ref, out_ref, wide, buffer):
    step = pl.program_id(0)
    rows = x_ref.shape[0]
    peers = pl.num_programs(0) * lists
    sections = hub_ref.shape[0] // peers

    @pl.when(step == 0)
    def _():
        wide[pl.ds(0, PAD), :] = jnp.zeros((PAD, wide.shape[1]), F32)
        wide[pl.ds(PAD, rows), :] = x_ref[...].astype(F32)

    for k in range(lists):
        peer = step * lists + k
        start = peer * slots
        buffer[...] = jnp.zeros_like(buffer)
        for section in range(sections):
            row = hub_ref[section * peers + peer]
            buffer[slots + section : slots + section + 1, :] = wide[pl.ds(row + PAD, 1), :]

        def body(group, carry):
            base = pl.multiple_of(group * UNROLL, UNROLL)
            for slot in range(UNROLL):
                row = list_ref[start + base + slot]
                buffer[pl.ds(base + slot, 1), :] = wide[pl.ds(row + PAD, 1), :]
            return carry

        lax.fori_loop(0, live_groups(list_ref, start, slots, UNROLL), body, 0)
        out_ref[k] = buffer[...].astype(BF)


def gather_rows(features, send_lists, hub_rows):
    peers, slots = send_lists.shape
    rows, width = features.shape
    lists = 8
    height = slots + PAD
    return pl.pallas_call(
        functools.partial(gather_kernel, lists, slots),
        grid_spec=pltpu.PrefetchScalarGridSpec(
            num_scalar_prefetch=2,
            grid=(peers // lists,),
            in_specs=[pl.BlockSpec((rows, width), lambda i, *_: (0, 0))],
            out_specs=pl.BlockSpec((lists, height, width), lambda i, *_: (i, 0, 0)),
            scratch_shapes=[
                pltpu.VMEM((rows + PAD, width), F32),
                pltpu.VMEM((height, width), F32),
            ],
        ),
        out_shape=jax.ShapeDtypeStruct((peers, height, width), BF),
        compiler_params=pltpu.CompilerParams(vmem_limit_bytes=10 * MIB),
    )(send_lists.reshape(-1), hub_rows.reshape(-1), features)


def tiles_kernel(group, columns_ref, x_hbm, halo_hbm, tiles_ref, z_ref, features, sems):
    step = pl.program_id(0)
    per_block, blk = tiles_ref.shape[1:3]
    own_blocks = x_hbm.shape[0]
    peers = halo_hbm.shape[0]

    @pl.when(step == 0)
    def _():
        own = pltpu.make_async_copy(x_hbm, features.at[pl.ds(0, own_blocks)], sems.at[0])
        halo = pltpu.make_async_copy(
            halo_hbm.at[:, pl.ds(0, blk), :], features.at[pl.ds(own_blocks, peers)], sems.at[1]
        )
        own.start()
        halo.start()
        own.wait()
        halo.wait()

    for u in range(group):
        places = [columns_ref[(step * group + u) * per_block + t] for t in range(per_block)]
        slab = jnp.concatenate([tiles_ref[u, t] for t in range(per_block)], axis=1)
        blocks = jnp.concatenate([features[place] for place in places], axis=0)
        z_ref[pl.ds(u * blk, blk), :] = jnp.dot(slab, blocks, preferred_element_type=F32)


def tiles_part(features, halo, tiles, tile_columns):
    blocks, per_block, blk, _ = tiles.shape
    peers = halo.shape[0]
    width = features.shape[1]
    group = 8
    return pl.pallas_call(
        functools.partial(tiles_kernel, group),
        grid_spec=pltpu.PrefetchScalarGridSpec(
            num_scalar_prefetch=1,
            grid=(blocks // group,),
            in_specs=[
                pl.BlockSpec(memory_space=pl.ANY),
                pl.BlockSpec(memory_space=pl.ANY),
                pl.BlockSpec((group, per_block, blk, blk), lambda i, *_: (i, 0, 0, 0)),
            ],
            out_specs=pl.BlockSpec((group * blk, width), lambda i, *_: (i, 0)),
            scratch_shapes=[
                pltpu.VMEM((blocks + peers, blk, width), BF),
                pltpu.SemaphoreType.DMA((2,)),
            ],
        ),
        out_shape=jax.ShapeDtypeStruct((blocks * blk, width), F32),
        compiler_params=pltpu.CompilerParams(vmem_limit_bytes=14 * MIB),
    )(tile_columns.reshape(-1), features.reshape(blocks, blk, width), halo, tiles)


def layer_kernel(
    group,
    steps,
    columns_ref,
    z_ref,
    hub_ref,
    w_ref,
    tiles_ref,
    hub_tiles_ref,
    cot_ref,
    out_ref,
    send_ref,
    own_ref,
    adjoint,
    hub_adjoint,
    grad_w,
    extra,
):
    step = pl.program_id(0)
    per_block, blk = tiles_ref.shape[1:3]
    sections = hub_tiles_ref.shape[0]
    width = hub_ref.shape[1]
    own_part = own_ref.shape[0] // blk
    send_part = send_ref.shape[0]
    finals = pl.num_programs(0) - steps
    own_blocks = finals * own_part

    @pl.when(step == 0)
    def _():
        def clear(block, carry):
            adjoint[block] = jnp.zeros((blk, width), F32)
            return carry

        lax.fori_loop(0, adjoint.shape[0], clear, 0, unroll=4)
        hub_adjoint[...] = jnp.zeros_like(hub_adjoint)
        grad_w[...] = jnp.zeros_like(grad_w)

    @pl.when(step < steps)
    def _():
        weight = w_ref[...]
        weight_twice = jnp.concatenate([weight, weight], axis=0)
        hub_slab = jnp.concatenate([hub_tiles_ref[s] for s in range(sections)], axis=1)
        z = z_ref[...] + jnp.dot(hub_slab, hub_ref[...], preferred_element_type=F32)
        z_high = z.astype(BF)
        z_low = (z - z_high.astype(F32)).astype(BF)
        preact = jnp.dot(
            jnp.concatenate([z_high, z_low], axis=1), weight_twice, preferred_element_type=F32
        )
        square = preact * preact
        t = jnp.tanh(preact * (GELU_A + (GELU_A * GELU_B) * square))
        half = 0.5 + 0.5 * t
        out_ref[...] = (preact * half).astype(BF)
        slope = half + (0.5 * preact) * (1.0 - t * t) * (GELU_A + (3.0 * GELU_A * GELU_B) * square)
        grad = (cot_ref[...].astype(F32) * slope).astype(BF)
        grad_w[...] += lax.dot_general(
            z_high, grad, (((0,), (0,)), ((), ())), preferred_element_type=F32
        )
        back = lax.dot_general(
            grad, weight, (((1,), (1,)), ((), ())), preferred_element_type=F32
        ).astype(BF)
        hub_adjoint[...] += lax.dot_general(
            hub_slab, back, (((0,), (0,)), ((), ())), preferred_element_type=F32
        )
        for u in range(group):
            places = [columns_ref[(step * group + u) * per_block + t] for t in range(per_block)]
            slab = jnp.concatenate([tiles_ref[u, t] for t in range(per_block)], axis=1)
            spread = lax.dot_general(
                slab,
                back[u * blk : (u + 1) * blk],
                (((0,), (0,)), ((), ())),
                preferred_element_type=F32,
            )
            for t in range(per_block):
                adjoint[places[t]] += spread[t * blk : (t + 1) * blk]

    @pl.when(step == steps)
    def _():
        for s in range(sections):
            extra[:, s, :] = hub_adjoint[s * blk : (s + 1) * blk, :]
        total = grad_w[...]
        high = total.astype(BF).astype(F32)
        low = total - high
        pieces = total.shape[1] // width
        for piece in range(pieces):
            part = slice(piece * width, (piece + 1) * width)
            extra[:, sections + piece, :] = high[:, part]
            extra[:, sections + pieces + piece, :] = low[:, part]

    @pl.when(step >= steps)
    def _():
        final = step - steps
        for block in range(own_part):
            own_ref[pl.ds(block * blk, blk), :] = adjoint[final * own_part + block]

        def finish(k, carry):
            peer = final * send_part + k
            rows = jnp.concatenate([adjoint[own_blocks + peer], extra[peer]], axis=0)
            send_ref[k] = rows.astype(BF)
            return carry

        lax.fori_loop(0, send_part, finish, 0, unroll=4)


def layer(z, hub, weight, tiles, tile_columns, hub_tiles, cotangent, peers):
    blocks, per_block, blk, _ = tiles.shape
    width, width_out = weight.shape
    sections = hub_tiles.shape[0]
    rows = blocks * blk
    group = 8
    steps = blocks // group
    finals = 4
    extras = sections + 2 * (width_out // width)

    def work(i):
        return jnp.minimum(i, steps - 1)

    def final(i):
        return jnp.maximum(i - steps, 0)

    return pl.pallas_call(
        functools.partial(layer_kernel, group, steps),
        grid_spec=pltpu.PrefetchScalarGridSpec(
            num_scalar_prefetch=1,
            grid=(steps + finals,),
            in_specs=[
                pl.BlockSpec((group * blk, width), lambda i, *_: (work(i), 0)),
                pl.BlockSpec((sections * blk, width), lambda i, *_: (0, 0)),
                pl.BlockSpec((width, width_out), lambda i, *_: (0, 0)),
                pl.BlockSpec((group, per_block, blk, blk), lambda i, *_: (work(i), 0, 0, 0)),
                pl.BlockSpec((sections, group * blk, blk), lambda i, *_: (0, work(i), 0)),
                pl.BlockSpec((group * blk, width_out), lambda i, *_: (work(i), 0)),
            ],
            out_specs=[
                pl.BlockSpec((group * blk, width_out), lambda i, *_: (work(i), 0)),
                pl.BlockSpec((peers // finals, blk + extras, width), lambda i, *_: (final(i), 0, 0)),
                pl.BlockSpec((rows // finals, width), lambda i, *_: (final(i), 0)),
            ],
            scratch_shapes=[
                pltpu.VMEM((blocks + peers, blk, width), F32),
                pltpu.VMEM((sections * blk, width), F32),
                pltpu.VMEM((width, width_out), F32),
                pltpu.VMEM((peers, extras, width), F32),
            ],
        ),
        out_shape=[
            jax.ShapeDtypeStruct((rows, width_out), BF),
            jax.ShapeDtypeStruct((peers, blk + extras, width), BF),
            jax.ShapeDtypeStruct((rows, width), F32),
        ],
        compiler_params=pltpu.CompilerParams(vmem_limit_bytes=32 * MIB),
    )(tile_columns.reshape(-1), z, hub, weight, tiles, hub_tiles, cotangent)


def scatter_kernel(lists, list_ref, back_ref, own_ref, out_ref, t0, t1, t2, t3, buffer):
    step = pl.program_id(0)
    steps = pl.num_programs(0)
    totals = (t0, t1, t2, t3)
    slots = buffer.shape[0]
    rows = own_ref.shape[0]

    @pl.when(step == 0)
    def _():
        for total in totals:
            total[...] = jnp.zeros_like(total)

    for k in range(lists):
        start = (step * lists + k) * slots
        buffer[...] = back_ref[k, :slots, :].astype(F32)

        def body(group, carry):
            base = pl.multiple_of(group * UNROLL, UNROLL)
            for slot in range(0, UNROLL, 4):
                places = [list_ref[start + base + slot + v] + PAD for v in range(4)]
                sums = [
                    totals[v][pl.ds(places[v], 1), :] + buffer[pl.ds(base + slot + v, 1), :]
                    for v in range(4)
                ]
                for v in range(4):
                    totals[v][pl.ds(places[v], 1), :] = sums[v]
            return carry

        lax.fori_loop(0, live_groups(list_ref, start, slots, UNROLL), body, 0)

    @pl.when(step == steps - 1)
    def _():
        live = pl.ds(PAD, rows)
        out_ref[...] = ((t0[live, :] + t1[live, :]) + (t2[live, :] + t3[live, :])) + own_ref[...]


def scatter_rows(send_lists, returned, own):
    peers, slots = send_lists.shape
    rows, width = own.shape
    lists = 8
    return pl.pallas_call(
        functools.partial(scatter_kernel, lists),
        grid_spec=pltpu.PrefetchScalarGridSpec(
            num_scalar_prefetch=1,
            grid=(peers // lists,),
            in_specs=[
                pl.BlockSpec((lists, returned.shape[1], width), lambda i, *_: (i, 0, 0)),
                pl.BlockSpec((rows, width), lambda i, *_: (0, 0)),
            ],
            out_specs=pl.BlockSpec((rows, width), lambda i, *_: (0, 0)),
            scratch_shapes=[pltpu.VMEM((rows + PAD, width), F32)] * 4
            + [pltpu.VMEM((slots, width), F32)],
        ),
        out_shape=jax.ShapeDtypeStruct((rows, width), F32),
        compiler_params=pltpu.CompilerParams(vmem_limit_bytes=24 * MIB),
    )(send_lists.reshape(-1), returned, own)


def finish_kernel(owned_ref, rows_ref, hub_ref, total_ref, out_ref, total):
    sections, peers, _ = hub_ref.shape
    total[...] = total_ref[...]
    group = 16
    for section in range(sections):

        @pl.when(owned_ref[section] != 0)
        def _():
            def body(step, carry):
                first = pl.multiple_of(step * group, group)
                for slot in range(group):
                    row = rows_ref[section * peers + first + slot]
                    total[pl.ds(row, 1), :] += hub_ref[section, pl.ds(first + slot, 1), :]
                return carry

            lax.fori_loop(0, peers // group, body, 0)

    out_ref[...] = total[...].astype(BF)


def finish(total, hub_sums, hub_rows, owned):
    rows, width = total.shape
    sections, peers, _ = hub_sums.shape
    return pl.pallas_call(
        finish_kernel,
        grid_spec=pltpu.PrefetchScalarGridSpec(
            num_scalar_prefetch=2,
            grid=(1,),
            in_specs=[
                pl.BlockSpec((sections, peers, width), lambda i, *_: (0, 0, 0)),
                pl.BlockSpec((rows, width), lambda i, *_: (0, 0)),
            ],
            out_specs=pl.BlockSpec((rows, width), lambda i, *_: (0, 0)),
            scratch_shapes=[pltpu.VMEM((rows, width), F32)],
        ),
        out_shape=jax.ShapeDtypeStruct((rows, width), BF),
        compiler_params=pltpu.CompilerParams(vmem_limit_bytes=12 * MIB),
    )(owned.astype(jnp.int32), hub_rows.reshape(-1), hub_sums, total)


def exchange(array):
    return lax.all_to_all(array, "rows", split_axis=0, concat_axis=0, tiled=True)


def body(
    features,
    weight,
    adjacency_tiles,
    tile_columns,
    send_rows,
    hub_owner,
    hub_rows,
    hub_tiles,
    cotangent,
):
    device = lax.axis_index("rows")
    sections, peers = hub_rows.shape
    width, width_out = weight.shape
    pieces = width_out // width
    send_lists = send_rows[0]

    blk = send_lists.shape[1]
    halo = exchange(gather_rows(features, send_lists, hub_rows))
    hub_mine = halo[hub_owner, blk + jnp.arange(sections)]
    hub_all = exchange(jnp.broadcast_to(hub_mine[None], (peers, sections, width)))
    hub = hub_all.transpose(1, 0, 2).reshape(sections * peers, width)
    z = tiles_part(features, halo, adjacency_tiles, tile_columns)
    output, adjoint, own = layer(
        z, hub, weight, adjacency_tiles, tile_columns, hub_tiles, cotangent, peers
    )
    returned = exchange(adjoint)

    sums = jnp.sum(returned[:, blk:, :].astype(F32), axis=0)
    weight_row = sums[sections : sections + pieces] + sums[sections + pieces :]
    high = weight_row.astype(BF)
    low = (weight_row - high.astype(F32)).astype(BF)
    mine = jnp.concatenate([sums[:sections].astype(BF), high, low], axis=0)
    everyone = exchange(jnp.broadcast_to(mine[None], (peers,) + mine.shape)).astype(F32)

    total = scatter_rows(send_lists, returned, own)
    hub_sums = everyone[:, :sections].transpose(1, 0, 2)
    grad_weight = everyone[:, sections : sections + pieces] + everyone[:, sections + pieces :]
    grad_features = finish(total, hub_sums, hub_rows, hub_owner == device)
    return (output, grad_features, grad_weight.reshape(width, width_out))


def solution(mesh):
    return jax.shard_map(
        body,
        mesh=mesh,
        in_specs=(
            P("rows", None),
            P(),
            P("rows", None, None, None),
            P("rows", None),
            P("rows", None, None),
            P(),
            P(),
            P(None, "rows", None),
            P("rows", None),
        ),
        out_specs=(P("rows", None), P("rows", None), P()),
        check_vma=False,
    )
```

```python
import functools

import jax
import jax.numpy as jnp
from jax import lax
from jax.experimental import pallas as pl
from jax.experimental.pallas import tpu as pltpu
from jax.sharding import PartitionSpec as P

BF = jnp.bfloat16
F32 = jnp.float32
VMEM_LIMIT = 60 * 2**20
PAD = 8
EXTRA = 8
FIRST_OUT = 32
FIRST_BACK = 80
GELU_A = 0.7978845608028654
GELU_B = 0.044715


def live_groups(list_ref, start, first, stop, group):
    count = jnp.int32(0)
    for slot in range(first, stop, group):
        count = count + (list_ref[start + slot] >= 0).astype(jnp.int32)
    return count


def gather_kernel(lists, slots, first, stop, list_ref, hub_ref, x_ref, out_ref, wide, buffer):
    step = pl.program_id(0)
    rows = x_ref.shape[0]
    peers = pl.num_programs(0) * lists
    sections = hub_ref.shape[0] // peers
    count = stop - first
    group = 16

    @pl.when(step == 0)
    def _():
        wide[pl.ds(0, PAD), :] = jnp.zeros((PAD, wide.shape[1]), F32)
        wide[pl.ds(PAD, rows), :] = x_ref[...].astype(F32)
        buffer[pl.ds(count, EXTRA), :] = jnp.zeros((EXTRA, wide.shape[1]), F32)

    def one_list(k, carry):
        peer = step * lists + k
        start = peer * slots
        if first == 0:
            for slot in range(count):
                row = list_ref[start + slot]
                buffer[slot : slot + 1, :] = wide[pl.ds(row + PAD, 1), :]
            for section in range(sections):
                row = hub_ref[section * peers + peer]
                buffer[count + section : count + section + 1, :] = wide[pl.ds(row + PAD, 1), :]
        else:
            buffer[pl.ds(0, count), :] = jnp.zeros((count, wide.shape[1]), F32)

            def body(part, carry):
                base = pl.multiple_of(part * group, group)
                for slot in range(group):
                    row = list_ref[start + first + base + slot]
                    buffer[pl.ds(base + slot, 1), :] = wide[pl.ds(row + PAD, 1), :]
                return carry

            lax.fori_loop(0, live_groups(list_ref, start, first, stop, group), body, 0)
        out_ref[k] = buffer[...].astype(BF)
        return carry

    lax.fori_loop(0, lists, one_list, 0, unroll=2 if first == 0 else 1)


def gather_rows(features, send_lists, hub_rows, first, stop):
    peers, slots = send_lists.shape
    rows, width = features.shape
    lists = 32
    height = stop - first + EXTRA
    return pl.pallas_call(
        functools.partial(gather_kernel, lists, slots, first, stop),
        grid_spec=pltpu.PrefetchScalarGridSpec(
            num_scalar_prefetch=2,
            grid=(peers // lists,),
            in_specs=[pl.BlockSpec((rows, width), lambda i, *_: (0, 0))],
            out_specs=pl.BlockSpec((lists, height, width), lambda i, *_: (i, 0, 0)),
            scratch_shapes=[
                pltpu.VMEM((rows + PAD, width), F32),
                pltpu.VMEM((height, width), F32),
            ],
        ),
        out_shape=jax.ShapeDtypeStruct((peers, height, width), BF),
        compiler_params=pltpu.CompilerParams(vmem_limit_bytes=VMEM_LIMIT),
    )(send_lists.reshape(-1), hub_rows.reshape(-1), features)


def layer_kernel(
    group,
    steps,
    columns_ref,
    x_hbm,
    halo1_hbm,
    halo2_hbm,
    hub_ref,
    w_ref,
    tiles_ref,
    hub_tiles_ref,
    cot_ref,
    out_ref,
    send1_ref,
    send2_ref,
    own_ref,
    features,
    adjoint,
    hub_adjoint,
    grad_w,
    extra,
    sems,
):
    step = pl.program_id(0)
    per_block, blk = tiles_ref.shape[1:3]
    sections = hub_tiles_ref.shape[0]
    width = hub_ref.shape[1]
    own_part = own_ref.shape[0] // blk
    send_part = send1_ref.shape[0]
    own_blocks = x_hbm.shape[0]
    peers = halo1_hbm.shape[0]
    slots1 = halo1_hbm.shape[1] - EXTRA
    back1 = send1_ref.shape[1] - EXTRA

    @pl.when(step == 0)
    def _():
        halo = pl.ds(own_blocks, peers)
        copies = [
            pltpu.make_async_copy(x_hbm, features.at[pl.ds(0, own_blocks)], sems.at[0]),
            pltpu.make_async_copy(
                halo1_hbm.at[:, pl.ds(0, slots1), :],
                features.at[halo, pl.ds(0, slots1), :],
                sems.at[1],
            ),
            pltpu.make_async_copy(
                halo2_hbm.at[:, pl.ds(0, blk - slots1), :],
                features.at[halo, pl.ds(slots1, blk - slots1), :],
                sems.at[2],
            ),
        ]
        for copy in copies:
            copy.start()

        def clear(block, carry):
            adjoint[block] = jnp.zeros((blk, width), F32)
            return carry

        lax.fori_loop(0, adjoint.shape[0], clear, 0, unroll=4)
        hub_adjoint[...] = jnp.zeros_like(hub_adjoint)
        grad_w[...] = jnp.zeros_like(grad_w)
        for copy in copies:
            copy.wait()

    @pl.when(step < steps)
    def _():
        weight = w_ref[...]
        weight_twice = jnp.concatenate([weight, weight], axis=0)
        hub_slab = jnp.concatenate([hub_tiles_ref[s] for s in range(sections)], axis=1)
        places = []
        slabs = []
        tiled = []
        for u in range(group):
            first = (step * group + u) * per_block
            places.append([columns_ref[first + t] for t in range(per_block)])
            slabs.append(jnp.concatenate([tiles_ref[u, t] for t in range(per_block)], axis=1))
            blocks = jnp.concatenate([features[place] for place in places[u]], axis=0)
            tiled.append(jnp.dot(slabs[u], blocks, preferred_element_type=F32))
        z = jnp.concatenate(tiled, axis=0)
        z = z + jnp.dot(hub_slab, hub_ref[...], preferred_element_type=F32)
        z_high = z.astype(BF)
        z_low = (z - z_high.astype(F32)).astype(BF)
        preact = jnp.dot(
            jnp.concatenate([z_high, z_low], axis=1), weight_twice, preferred_element_type=F32
        )
        square = preact * preact
        t = jnp.tanh(preact * (GELU_A + (GELU_A * GELU_B) * square))
        half = 0.5 + 0.5 * t
        out_ref[...] = (preact * half).astype(BF)
        slope = half + (0.5 * preact) * (1.0 - t * t) * (GELU_A + (3.0 * GELU_A * GELU_B) * square)
        grad = (cot_ref[...].astype(F32) * slope).astype(BF)
        grad_w[...] += lax.dot_general(
            z_high, grad, (((0,), (0,)), ((), ())), preferred_element_type=F32
        )
        back = lax.dot_general(
            grad, weight, (((1,), (1,)), ((), ())), preferred_element_type=F32
        ).astype(BF)
        hub_adjoint[...] += lax.dot_general(
            hub_slab, back, (((0,), (0,)), ((), ())), preferred_element_type=F32
        )
        for u in range(group):
            spread = lax.dot_general(
                slabs[u],
                back[u * blk : (u + 1) * blk],
                (((0,), (0,)), ((), ())),
                preferred_element_type=F32,
            )
            for t in range(per_block):
                adjoint[places[u][t]] += spread[t * blk : (t + 1) * blk]

    @pl.when(step == steps)
    def _():
        for s in range(sections):
            extra[:, s, :] = hub_adjoint[s * blk : (s + 1) * blk, :]
        total = grad_w[...]
        high = total.astype(BF).astype(F32)
        low = total - high
        pieces = total.shape[1] // width
        for piece in range(pieces):
            part = slice(piece * width, (piece + 1) * width)
            extra[:, sections + piece, :] = high[:, part]
            extra[:, sections + pieces + piece, :] = low[:, part]

    @pl.when(step >= steps)
    def _():
        final = step - steps
        for block in range(own_part):
            own_ref[pl.ds(block * blk, blk), :] = adjoint[final * own_part + block]

        def finish(k, carry):
            peer = final * send_part + k
            rows = adjoint[own_blocks + peer]
            tail = extra[peer]
            send1_ref[k] = jnp.concatenate([rows[:back1], tail], axis=0).astype(BF)
            send2_ref[k] = jnp.concatenate([rows[back1:], tail], axis=0).astype(BF)
            return carry

        lax.fori_loop(0, send_part, finish, 0, unroll=4)


def layer(features, halo1, halo2, hub, weight, tiles, tile_columns, hub_tiles, cotangent):
    blocks, per_block, blk, _ = tiles.shape
    width, width_out = weight.shape
    sections = hub_tiles.shape[0]
    peers = halo1.shape[0]
    rows = blocks * blk
    group = 8
    steps = blocks // group
    finals = 4
    height1 = FIRST_BACK + EXTRA
    height2 = blk - FIRST_BACK + EXTRA

    def work(i):
        return jnp.minimum(i, steps - 1)

    def final(i):
        return jnp.maximum(i - steps, 0)

    return pl.pallas_call(
        functools.partial(layer_kernel, group, steps),
        grid_spec=pltpu.PrefetchScalarGridSpec(
            num_scalar_prefetch=1,
            grid=(steps + finals,),
            in_specs=[
                pl.BlockSpec(memory_space=pl.ANY),
                pl.BlockSpec(memory_space=pl.ANY),
                pl.BlockSpec(memory_space=pl.ANY),
                pl.BlockSpec((sections * blk, width), lambda i, *_: (0, 0)),
                pl.BlockSpec((width, width_out), lambda i, *_: (0, 0)),
                pl.BlockSpec((group, per_block, blk, blk), lambda i, *_: (work(i), 0, 0, 0)),
                pl.BlockSpec((sections, group * blk, blk), lambda i, *_: (0, work(i), 0)),
                pl.BlockSpec((group * blk, width_out), lambda i, *_: (work(i), 0)),
            ],
            out_specs=[
                pl.BlockSpec((group * blk, width_out), lambda i, *_: (work(i), 0)),
                pl.BlockSpec((peers // finals, height1, width), lambda i, *_: (final(i), 0, 0)),
                pl.BlockSpec((peers // finals, height2, width), lambda i, *_: (final(i), 0, 0)),
                pl.BlockSpec((rows // finals, width), lambda i, *_: (final(i), 0)),
            ],
            scratch_shapes=[
                pltpu.VMEM((blocks + peers, blk, width), BF),
                pltpu.VMEM((blocks + peers, blk, width), F32),
                pltpu.VMEM((sections * blk, width), F32),
                pltpu.VMEM((width, width_out), F32),
                pltpu.VMEM((peers, EXTRA, width), F32),
                pltpu.SemaphoreType.DMA((3,)),
            ],
        ),
        out_shape=[
            jax.ShapeDtypeStruct((rows, width_out), BF),
            jax.ShapeDtypeStruct((peers, height1, width), BF),
            jax.ShapeDtypeStruct((peers, height2, width), BF),
            jax.ShapeDtypeStruct((rows, width), F32),
        ],
        compiler_params=pltpu.CompilerParams(vmem_limit_bytes=VMEM_LIMIT),
    )(
        tile_columns.reshape(-1),
        features.reshape(blocks, blk, width),
        halo1,
        halo2,
        hub,
        weight,
        tiles,
        hub_tiles,
        cotangent,
    )


def scatter_kernel(
    lists, slots, first, stop, last, list_ref, hub_ref, back_ref, start_ref, out_ref, t0, t1, t2, t3, buffer
):
    step = pl.program_id(0)
    steps = pl.num_programs(0)
    totals = (t0, t1, t2, t3)
    rows, width = start_ref.shape
    peers = steps * lists
    sections = hub_ref.shape[0] // peers
    live = pl.ds(PAD, rows)
    group = 16

    @pl.when(step == 0)
    def _():
        t0[live, :] = start_ref[...]
        for total in totals[1:]:
            total[...] = jnp.zeros_like(total)

    def one_list(k, carry):
        peer = step * lists + k
        start = peer * slots
        buffer[...] = back_ref[k].astype(F32)

        def add(places, base):
            sums = [
                totals[v][pl.ds(place + PAD, 1), :] + buffer[pl.ds(base + v, 1), :]
                for v, place in enumerate(places)
            ]
            for v, place in enumerate(places):
                totals[v][pl.ds(place + PAD, 1), :] = sums[v]

        if last:
            for s in range(0, sections, 4):
                count = min(4, sections - s)
                add([hub_ref[(s + v) * peers + peer] for v in range(count)], stop - first + s)

        def body(part, carry):
            base = pl.multiple_of(part * group, group)
            for slot in range(0, group, 4):
                add([list_ref[start + first + base + slot + v] for v in range(4)], base + slot)
            return carry

        lax.fori_loop(0, live_groups(list_ref, start, first, stop, group), body, 0)
        return carry

    lax.fori_loop(0, lists, one_list, 0)

    @pl.when(step == steps - 1)
    def _():
        total = (t0[live, :] + t1[live, :]) + (t2[live, :] + t3[live, :])
        out_ref[...] = total.astype(out_ref.dtype)


def scatter_rows(send_lists, hub_places, returned, start, first, stop, last):
    peers, slots = send_lists.shape
    rows, width = start.shape
    lists = 32
    height = returned.shape[1]
    dtype = BF if last else F32
    return pl.pallas_call(
        functools.partial(scatter_kernel, lists, slots, first, stop, last),
        grid_spec=pltpu.PrefetchScalarGridSpec(
            num_scalar_prefetch=2,
            grid=(peers // lists,),
            in_specs=[
                pl.BlockSpec((lists, height, width), lambda i, *_: (i, 0, 0)),
                pl.BlockSpec((rows, width), lambda i, *_: (0, 0)),
            ],
            out_specs=pl.BlockSpec((rows, width), lambda i, *_: (0, 0)),
            scratch_shapes=[pltpu.VMEM((rows + PAD, width), F32)] * 4
            + [pltpu.VMEM((height, width), F32)],
        ),
        out_shape=jax.ShapeDtypeStruct((rows, width), dtype),
        compiler_params=pltpu.CompilerParams(vmem_limit_bytes=VMEM_LIMIT),
    )(send_lists.reshape(-1), hub_places.reshape(-1), returned, start)


def exchange(array):
    return lax.all_to_all(array, "rows", split_axis=0, concat_axis=0, tiled=True)


def body(
    features,
    weight,
    adjacency_tiles,
    tile_columns,
    send_rows,
    hub_owner,
    hub_rows,
    hub_tiles,
    cotangent,
):
    device = lax.axis_index("rows")
    sections, peers = hub_rows.shape
    width, width_out = weight.shape
    pieces = width_out // width
    send_lists = send_rows[0]
    slots = send_lists.shape[1]

    halo1 = exchange(gather_rows(features, send_lists, hub_rows, 0, FIRST_OUT))
    part = gather_rows(features, send_lists, hub_rows, FIRST_OUT, slots)
    hub_mine = halo1[hub_owner, FIRST_OUT + jnp.arange(sections)]
    end = slots - FIRST_OUT
    part = part.at[:, end : end + sections].set(
        jnp.broadcast_to(hub_mine[None], (peers, sections, width))
    )
    halo2 = exchange(part)
    hub = halo2[:, end : end + sections].transpose(1, 0, 2).reshape(sections * peers, width)

    output, send1, send2, own = layer(
        features, halo1, halo2, hub, weight, adjacency_tiles, tile_columns, hub_tiles, cotangent
    )

    back1 = exchange(send1)
    sums = jnp.sum(back1[:, FIRST_BACK:].astype(F32), axis=0)
    weight_row = sums[sections : sections + pieces] + sums[sections + pieces :]
    high = weight_row.astype(BF)
    low = (weight_row - high.astype(F32)).astype(BF)
    mine = jnp.concatenate([sums[:sections].astype(BF), high, low], axis=0)
    end = slots - FIRST_BACK
    send2 = send2.at[:, end:].set(jnp.broadcast_to(mine[None], (peers,) + mine.shape))
    back2 = exchange(send2)

    hub_places = jnp.where((hub_owner == device)[:, None], hub_rows, -1)
    total = scatter_rows(send_lists, hub_places, back1, own, 0, FIRST_BACK, False)
    grad_features = scatter_rows(send_lists, hub_places, back2, total, FIRST_BACK, slots, True)
    tail = back2[:, end + sections :].astype(F32)
    grad_weight = (tail[:, :pieces] + tail[:, pieces:]).reshape(width, width_out)
    return (output, grad_features, grad_weight)


def solution(mesh):
    return jax.shard_map(
        body,
        mesh=mesh,
        in_specs=(
            P("rows", None),
            P(),
            P("rows", None, None, None),
            P("rows", None),
            P("rows", None, None),
            P(),
            P(),
            P(None, "rows", None),
            P("rows", None),
        ),
        out_specs=(P("rows", None), P("rows", None), P()),
        check_vma=False,
    )
```

```python
import functools

import jax
import jax.numpy as jnp
from jax import lax
from jax.experimental import pallas as pl
from jax.experimental.pallas import tpu as pltpu
from jax.sharding import PartitionSpec as P

BF = jnp.bfloat16
F32 = jnp.float32
VMEM_LIMIT = 60 * 2**20
PAD = 8
EXTRA = 8
FIRST_OUT = 32
FIRST_BACK = 80
GELU_A = 0.7978845608028654
GELU_B = 0.044715


def each_live_group(list_ref, start, base, stop, group, work):
    if base < stop:

        @pl.when(list_ref[start + base] >= 0)
        def _():
            work(base)
            each_live_group(list_ref, start, base + group, stop, group, work)


def gather_kernel(lists, slots, first, stop, list_ref, hub_ref, x_ref, out_ref, wide, buffer):
    step = pl.program_id(0)
    rows = x_ref.shape[0]
    peers = pl.num_programs(0) * lists
    sections = hub_ref.shape[0] // peers
    count = stop - first
    group = 16

    @pl.when(step == 0)
    def _():
        wide[pl.ds(0, PAD), :] = jnp.zeros((PAD, wide.shape[1]), F32)
        wide[pl.ds(PAD, rows), :] = x_ref[...].astype(F32)
        buffer[pl.ds(count, EXTRA), :] = jnp.zeros((EXTRA, wide.shape[1]), F32)

    def one_list(k, carry):
        peer = step * lists + k
        start = peer * slots
        if first == 0:
            for slot in range(count):
                row = list_ref[start + slot]
                buffer[slot : slot + 1, :] = wide[pl.ds(row + PAD, 1), :]
            for section in range(sections):
                row = hub_ref[section * peers + peer]
                buffer[count + section : count + section + 1, :] = wide[pl.ds(row + PAD, 1), :]
        else:
            buffer[pl.ds(0, count), :] = jnp.zeros((count, wide.shape[1]), F32)

            def work(base):
                for slot in range(base, base + group):
                    row = list_ref[start + slot]
                    buffer[slot - first : slot - first + 1, :] = wide[pl.ds(row + PAD, 1), :]

            each_live_group(list_ref, start, first, stop, group, work)
        out_ref[k] = buffer[...].astype(BF)
        return carry

    lax.fori_loop(0, lists, one_list, 0, unroll=2 if first == 0 else 1)


def gather_rows(features, send_lists, hub_rows, first, stop):
    peers, slots = send_lists.shape
    rows, width = features.shape
    lists = 32
    height = stop - first + EXTRA
    return pl.pallas_call(
        functools.partial(gather_kernel, lists, slots, first, stop),
        grid_spec=pltpu.PrefetchScalarGridSpec(
            num_scalar_prefetch=2,
            grid=(peers // lists,),
            in_specs=[pl.BlockSpec((rows, width), lambda i, *_: (0, 0))],
            out_specs=pl.BlockSpec((lists, height, width), lambda i, *_: (i, 0, 0)),
            scratch_shapes=[
                pltpu.VMEM((rows + PAD, width), F32),
                pltpu.VMEM((height, width), F32),
            ],
        ),
        out_shape=jax.ShapeDtypeStruct((peers, height, width), BF),
        compiler_params=pltpu.CompilerParams(vmem_limit_bytes=VMEM_LIMIT),
    )(send_lists.reshape(-1), hub_rows.reshape(-1), features)


def layer_kernel(
    group,
    steps,
    columns_ref,
    x_hbm,
    halo1_hbm,
    halo2_hbm,
    hub_ref,
    w_ref,
    tiles_ref,
    hub_tiles_ref,
    cot_ref,
    out_ref,
    send1_ref,
    send2_ref,
    own_ref,
    features,
    adjoint,
    hub_adjoint,
    grad_w,
    extra,
    sems,
):
    step = pl.program_id(0)
    per_block, blk = tiles_ref.shape[1:3]
    sections = hub_tiles_ref.shape[0]
    width = hub_ref.shape[1]
    own_part = own_ref.shape[0] // blk
    send_part = send1_ref.shape[0]
    own_blocks = x_hbm.shape[0]
    peers = halo1_hbm.shape[0]
    slots1 = halo1_hbm.shape[1] - EXTRA
    back1 = send1_ref.shape[1] - EXTRA

    @pl.when(step == 0)
    def _():
        halo = pl.ds(own_blocks, peers)
        copies = [
            pltpu.make_async_copy(x_hbm, features.at[pl.ds(0, own_blocks)], sems.at[0]),
            pltpu.make_async_copy(
                halo1_hbm.at[:, pl.ds(0, slots1), :],
                features.at[halo, pl.ds(0, slots1), :],
                sems.at[1],
            ),
            pltpu.make_async_copy(
                halo2_hbm.at[:, pl.ds(0, blk - slots1), :],
                features.at[halo, pl.ds(slots1, blk - slots1), :],
                sems.at[2],
            ),
        ]
        for copy in copies:
            copy.start()

        def clear(block, carry):
            adjoint[block] = jnp.zeros((blk, width), F32)
            return carry

        lax.fori_loop(0, adjoint.shape[0], clear, 0, unroll=4)
        hub_adjoint[...] = jnp.zeros_like(hub_adjoint)
        grad_w[...] = jnp.zeros_like(grad_w)
        for copy in copies:
            copy.wait()

    @pl.when(step < steps)
    def _():
        weight = w_ref[...]
        weight_twice = jnp.concatenate([weight, weight], axis=0)
        hub_slab = jnp.concatenate([hub_tiles_ref[s] for s in range(sections)], axis=1)
        places = []
        slabs = []
        tiled = []
        for u in range(group):
            first = (step * group + u) * per_block
            places.append([columns_ref[first + t] for t in range(per_block)])
            slabs.append(jnp.concatenate([tiles_ref[u, t] for t in range(per_block)], axis=1))
            blocks = jnp.concatenate([features[place] for place in places[u]], axis=0)
            tiled.append(jnp.dot(slabs[u], blocks, preferred_element_type=F32))
        z = jnp.concatenate(tiled, axis=0)
        z = z + jnp.dot(hub_slab, hub_ref[...], preferred_element_type=F32)
        z_high = z.astype(BF)
        z_low = (z - z_high.astype(F32)).astype(BF)
        preact = jnp.dot(
            jnp.concatenate([z_high, z_low], axis=1), weight_twice, preferred_element_type=F32
        )
        square = preact * preact
        t = jnp.tanh(preact * (GELU_A + (GELU_A * GELU_B) * square))
        half = 0.5 + 0.5 * t
        out_ref[...] = (preact * half).astype(BF)
        slope = half + (0.5 * preact) * (1.0 - t * t) * (GELU_A + (3.0 * GELU_A * GELU_B) * square)
        grad = (cot_ref[...].astype(F32) * slope).astype(BF)
        grad_w[...] += lax.dot_general(
            z_high, grad, (((0,), (0,)), ((), ())), preferred_element_type=F32
        )
        back = lax.dot_general(
            grad, weight, (((1,), (1,)), ((), ())), preferred_element_type=F32
        ).astype(BF)
        back_turned = lax.dot_general(
            weight, grad, (((1,), (1,)), ((), ())), preferred_element_type=F32
        ).astype(BF)
        hub_adjoint[...] += jnp.dot(back_turned, hub_slab, preferred_element_type=F32)
        for u in range(group):
            spread = lax.dot_general(
                slabs[u],
                back[u * blk : (u + 1) * blk],
                (((0,), (0,)), ((), ())),
                preferred_element_type=F32,
            )
            for t in range(per_block):
                adjoint[places[u][t]] += spread[t * blk : (t + 1) * blk]

    @pl.when(step == steps)
    def _():
        for s in range(sections):
            extra[:, s, :] = hub_adjoint[:, s * blk : (s + 1) * blk].T
        total = grad_w[...]
        high = total.astype(BF).astype(F32)
        low = total - high
        pieces = total.shape[1] // width
        for piece in range(pieces):
            part = slice(piece * width, (piece + 1) * width)
            extra[:, sections + piece, :] = high[:, part]
            extra[:, sections + pieces + piece, :] = low[:, part]

    @pl.when(step >= steps)
    def _():
        final = step - steps
        for block in range(own_part):
            own_ref[pl.ds(block * blk, blk), :] = adjoint[final * own_part + block]

        def finish(k, carry):
            peer = final * send_part + k
            rows = adjoint[own_blocks + peer]
            tail = extra[peer]
            send1_ref[k] = jnp.concatenate([rows[:back1], tail], axis=0).astype(BF)
            send2_ref[k] = jnp.concatenate([rows[back1:], tail], axis=0).astype(BF)
            return carry

        lax.fori_loop(0, send_part, finish, 0, unroll=4)


def layer(features, halo1, halo2, hub, weight, tiles, tile_columns, hub_tiles, cotangent):
    blocks, per_block, blk, _ = tiles.shape
    width, width_out = weight.shape
    sections = hub_tiles.shape[0]
    peers = halo1.shape[0]
    rows = blocks * blk
    group = 8
    steps = blocks // group
    finals = 4
    height1 = FIRST_BACK + EXTRA
    height2 = blk - FIRST_BACK + EXTRA

    def work(i):
        return jnp.minimum(i, steps - 1)

    def final(i):
        return jnp.maximum(i - steps, 0)

    return pl.pallas_call(
        functools.partial(layer_kernel, group, steps),
        grid_spec=pltpu.PrefetchScalarGridSpec(
            num_scalar_prefetch=1,
            grid=(steps + finals,),
            in_specs=[
                pl.BlockSpec(memory_space=pl.ANY),
                pl.BlockSpec(memory_space=pl.ANY),
                pl.BlockSpec(memory_space=pl.ANY),
                pl.BlockSpec((sections * blk, width), lambda i, *_: (0, 0)),
                pl.BlockSpec((width, width_out), lambda i, *_: (0, 0)),
                pl.BlockSpec((group, per_block, blk, blk), lambda i, *_: (work(i), 0, 0, 0)),
                pl.BlockSpec((sections, group * blk, blk), lambda i, *_: (0, work(i), 0)),
                pl.BlockSpec((group * blk, width_out), lambda i, *_: (work(i), 0)),
            ],
            out_specs=[
                pl.BlockSpec((group * blk, width_out), lambda i, *_: (work(i), 0)),
                pl.BlockSpec((peers // finals, height1, width), lambda i, *_: (final(i), 0, 0)),
                pl.BlockSpec((peers // finals, height2, width), lambda i, *_: (final(i), 0, 0)),
                pl.BlockSpec((rows // finals, width), lambda i, *_: (final(i), 0)),
            ],
            scratch_shapes=[
                pltpu.VMEM((blocks + peers, blk, width), BF),
                pltpu.VMEM((blocks + peers, blk, width), F32),
                pltpu.VMEM((width, sections * blk), F32),
                pltpu.VMEM((width, width_out), F32),
                pltpu.VMEM((peers, EXTRA, width), F32),
                pltpu.SemaphoreType.DMA((3,)),
            ],
        ),
        out_shape=[
            jax.ShapeDtypeStruct((rows, width_out), BF),
            jax.ShapeDtypeStruct((peers, height1, width), BF),
            jax.ShapeDtypeStruct((peers, height2, width), BF),
            jax.ShapeDtypeStruct((rows, width), F32),
        ],
        compiler_params=pltpu.CompilerParams(vmem_limit_bytes=VMEM_LIMIT),
    )(
        tile_columns.reshape(-1),
        features.reshape(blocks, blk, width),
        halo1,
        halo2,
        hub,
        weight,
        tiles,
        hub_tiles,
        cotangent,
    )


def add_rows(totals, places, buffer, base):
    sums = [
        totals[v][pl.ds(place + PAD, 1), :] + buffer[pl.ds(base + v, 1), :]
        for v, place in enumerate(places)
    ]
    for v, place in enumerate(places):
        totals[v][pl.ds(place + PAD, 1), :] = sums[v]


def begin_totals(totals, start_ref):
    totals[0][pl.ds(PAD, start_ref.shape[0]), :] = start_ref[...]
    for total in totals[1:]:
        total[...] = jnp.zeros_like(total)


def sum_totals(totals, rows):
    live = pl.ds(PAD, rows)
    t0, t1, t2, t3 = totals
    return (t0[live, :] + t1[live, :]) + (t2[live, :] + t3[live, :])


def scatter_kernel(lists, slots, stop, list_ref, back_ref, start_ref, out_ref, t0, t1, t2, t3, buffer):
    step = pl.program_id(0)
    totals = (t0, t1, t2, t3)
    group = 16

    @pl.when(step == 0)
    def _():
        begin_totals(totals, start_ref)

    def one_list(k, carry):
        start = (step * lists + k) * slots
        buffer[...] = back_ref[k].astype(F32)

        def work(base):
            for slot in range(base, base + group, 4):
                places = [list_ref[start + slot + v] for v in range(4)]
                add_rows(totals, places, buffer, slot)

        for base in range(0, 32, group):
            work(base)
        each_live_group(list_ref, start, 32, stop, group, work)
        return carry

    lax.fori_loop(0, lists, one_list, 0)

    @pl.when(step == pl.num_programs(0) - 1)
    def _():
        out_ref[...] = sum_totals(totals, start_ref.shape[0])


def scatter_first(send_lists, returned, start):
    peers, slots = send_lists.shape
    rows, width = start.shape
    lists = 32
    height = returned.shape[1]
    return pl.pallas_call(
        functools.partial(scatter_kernel, lists, slots, height - EXTRA),
        grid_spec=pltpu.PrefetchScalarGridSpec(
            num_scalar_prefetch=1,
            grid=(peers // lists,),
            in_specs=[
                pl.BlockSpec((lists, height, width), lambda i, *_: (i, 0, 0)),
                pl.BlockSpec((rows, width), lambda i, *_: (0, 0)),
            ],
            out_specs=pl.BlockSpec((rows, width), lambda i, *_: (0, 0)),
            scratch_shapes=[pltpu.VMEM((rows + PAD, width), F32)] * 4
            + [pltpu.VMEM((height, width), F32)],
        ),
        out_shape=jax.ShapeDtypeStruct((rows, width), F32),
        compiler_params=pltpu.CompilerParams(vmem_limit_bytes=VMEM_LIMIT),
    )(send_lists.reshape(-1), returned, start)


def last_kernel(
    sections,
    list_ref,
    hub_ref,
    owned_ref,
    back_ref,
    start_ref,
    out_ref,
    grad_w_ref,
    t0,
    t1,
    t2,
    t3,
    buffer,
    grad_w,
):
    totals = (t0, t1, t2, t3)
    peers, height, width = back_ref.shape
    count = height - EXTRA
    group = 16
    pieces = grad_w_ref.shape[1] // width
    begin_totals(totals, start_ref)

    def widen(part, carry):
        for k in range(8):
            peer = part * 8 + k
            buffer[peer] = back_ref[peer].astype(F32)
            for piece in range(pieces):
                high = count + sections + piece
                low = high + pieces
                grad_w[piece, pl.ds(peer, 1), :] = (
                    buffer[peer, high : high + 1, :] + buffer[peer, low : low + 1, :]
                )
        return carry

    lax.fori_loop(0, peers // 8, widen, 0)

    def one_list(peer, carry):
        rows = buffer.at[peer]

        def work(base):
            for slot in range(base, base + group, 4):
                places = [list_ref[peer * count + slot + v] for v in range(4)]
                add_rows(totals, places, rows, slot)

        each_live_group(list_ref, peer * count, 0, count, group, work)
        return carry

    lax.fori_loop(0, peers, one_list, 0, unroll=2)

    for section in range(sections):

        @pl.when(owned_ref[section] != 0)
        def _():
            def some_rows(part, carry):
                for k in range(0, group, 4):
                    for v in range(4):
                        peer = part * group + k + v
                        place = hub_ref[section * peers + peer] + PAD
                        row = buffer[peer, count + section : count + section + 1, :]
                        totals[v][pl.ds(place, 1), :] += row
                return carry

            lax.fori_loop(0, peers // group, some_rows, 0)

    for piece in range(pieces):
        grad_w_ref[:, piece * width : (piece + 1) * width] = grad_w[piece]
    out_ref[...] = sum_totals(totals, start_ref.shape[0]).astype(BF)


def scatter_last(send_lists, hub_rows, owned, returned, start, width_out):
    peers = send_lists.shape[0]
    rows, width = start.shape
    height = returned.shape[1]
    return pl.pallas_call(
        functools.partial(last_kernel, hub_rows.shape[0]),
        grid_spec=pltpu.PrefetchScalarGridSpec(
            num_scalar_prefetch=3,
            grid=(1,),
            in_specs=[
                pl.BlockSpec((peers, height, width), lambda i, *_: (0, 0, 0)),
                pl.BlockSpec((rows, width), lambda i, *_: (0, 0)),
            ],
            out_specs=[
                pl.BlockSpec((rows, width), lambda i, *_: (0, 0)),
                pl.BlockSpec((width, width_out), lambda i, *_: (0, 0)),
            ],
            scratch_shapes=[pltpu.VMEM((rows + PAD, width), F32)] * 4
            + [
                pltpu.VMEM((peers, height, width), F32),
                pltpu.VMEM((width_out // width, peers, width), F32),
            ],
        ),
        out_shape=[
            jax.ShapeDtypeStruct((rows, width), BF),
            jax.ShapeDtypeStruct((width, width_out), F32),
        ],
        compiler_params=pltpu.CompilerParams(vmem_limit_bytes=VMEM_LIMIT),
    )(send_lists.reshape(-1), hub_rows.reshape(-1), owned, returned, start)


def exchange(array):
    return lax.all_to_all(array, "rows", split_axis=0, concat_axis=0, tiled=True)


def body(
    features,
    weight,
    adjacency_tiles,
    tile_columns,
    send_rows,
    hub_owner,
    hub_rows,
    hub_tiles,
    cotangent,
):
    device = lax.axis_index("rows")
    sections, peers = hub_rows.shape
    width, width_out = weight.shape
    pieces = width_out // width
    send_lists = send_rows[0]
    slots = send_lists.shape[1]

    halo1 = exchange(gather_rows(features, send_lists, hub_rows, 0, FIRST_OUT))
    part = gather_rows(features, send_lists, hub_rows, FIRST_OUT, slots)
    hub_mine = halo1[hub_owner, FIRST_OUT + jnp.arange(sections)]
    end = slots - FIRST_OUT
    part = part.at[:, end : end + sections].set(
        jnp.broadcast_to(hub_mine[None], (peers, sections, width))
    )
    halo2 = exchange(part)
    hub = halo2[:, end : end + sections].transpose(1, 0, 2).reshape(sections * peers, width)

    output, send1, send2, own = layer(
        features, halo1, halo2, hub, weight, adjacency_tiles, tile_columns, hub_tiles, cotangent
    )

    back1 = exchange(send1)
    sums = jnp.sum(back1[:, FIRST_BACK:].astype(F32), axis=0)
    weight_row = sums[sections : sections + pieces] + sums[sections + pieces :]
    high = weight_row.astype(BF)
    low = (weight_row - high.astype(F32)).astype(BF)
    mine = jnp.concatenate([sums[:sections].astype(BF), high, low], axis=0)
    end = slots - FIRST_BACK
    send2 = send2.at[:, end:].set(jnp.broadcast_to(mine[None], (peers,) + mine.shape))
    back2 = exchange(send2)

    owned = (hub_owner == device).astype(jnp.int32)
    total = scatter_first(send_lists, back1, own)
    grad_features, grad_weight = scatter_last(
        send_lists[:, FIRST_BACK:], hub_rows, owned, back2, total, width_out
    )
    return (output, grad_features, grad_weight)


def solution(mesh):
    return jax.shard_map(
        body,
        mesh=mesh,
        in_specs=(
            P("rows", None),
            P(),
            P("rows", None, None, None),
            P("rows", None),
            P("rows", None, None),
            P(),
            P(),
            P(None, "rows", None),
            P("rows", None),
        ),
        out_specs=(P("rows", None), P("rows", None), P()),
        check_vma=False,
    )
```

```python
import functools

import jax
import jax.numpy as jnp
from jax import lax
from jax.experimental import pallas as pl
from jax.experimental.pallas import tpu as pltpu
from jax.sharding import PartitionSpec as P

BF = jnp.bfloat16
F32 = jnp.float32
VMEM_LIMIT = 60 * 2**20
LAYER_LIMIT = 50 * 2**20
PAD = 8
EXTRA = 8
HUBS = 4
FIRST_OUT = 36
LIVE = 32
FIRST_BACK = 80
GELU_A = 0.7978845608028654
GELU_B = 0.044715


def each_live_group(list_ref, start, base, stop, group, work):
    if base < stop:
        end = min(stop, (base // group + 1) * group)

        @pl.when(list_ref[start + base] >= 0)
        def _():
            work(base, end)
            each_live_group(list_ref, start, end, stop, group, work)


def gather_kernel(lists, slots, first, stop, list_ref, hub_ref, x_ref, out_ref, wide, buffer):
    step = pl.program_id(0)
    rows = x_ref.shape[0]
    peers = pl.num_programs(0) * lists
    sections = hub_ref.shape[0] // peers
    count = stop - first

    @pl.when(step == 0)
    def _():
        wide[pl.ds(0, PAD), :] = jnp.zeros((PAD, wide.shape[1]), F32)
        wide[pl.ds(PAD, rows), :] = x_ref[...].astype(F32)

    def one_list(k, carry):
        peer = step * lists + k
        start = peer * slots
        if first == 0:
            for slot in range(count):
                row = list_ref[start + slot]
                buffer[slot : slot + 1, :] = wide[pl.ds(row + PAD, 1), :]
            for section in range(sections):
                row = hub_ref[section * peers + peer]
                buffer[count + section : count + section + 1, :] = wide[pl.ds(row + PAD, 1), :]
        else:
            buffer[...] = jnp.zeros_like(buffer)

            def work(base, end):
                for slot in range(base, end):
                    row = list_ref[start + slot]
                    place = HUBS + slot - first
                    buffer[place : place + 1, :] = wide[pl.ds(row + PAD, 1), :]

            each_live_group(list_ref, start, first, stop, 16, work)
        out_ref[k] = buffer[...].astype(BF)
        return carry

    lax.fori_loop(0, lists, one_list, 0, unroll=2 if first == 0 else 1)


def gather_rows(features, send_lists, hub_rows, first, stop):
    peers, slots = send_lists.shape
    rows, width = features.shape
    lists = 32
    height = stop - first + HUBS
    return pl.pallas_call(
        functools.partial(gather_kernel, lists, slots, first, stop),
        grid_spec=pltpu.PrefetchScalarGridSpec(
            num_scalar_prefetch=2,
            grid=(peers // lists,),
            in_specs=[pl.BlockSpec((rows, width), lambda i, *_: (0, 0))],
            out_specs=pl.BlockSpec((lists, height, width), lambda i, *_: (i, 0, 0)),
            scratch_shapes=[
                pltpu.VMEM((rows + PAD, width), F32),
                pltpu.VMEM((height, width), F32),
            ],
        ),
        out_shape=jax.ShapeDtypeStruct((peers, height, width), BF),
        compiler_params=pltpu.CompilerParams(vmem_limit_bytes=VMEM_LIMIT),
    )(send_lists.reshape(-1), hub_rows.reshape(-1), features)


def layer_kernel(
    group,
    steps,
    columns_ref,
    x_hbm,
    halo1_ref,
    halo2_hbm,
    hub_ref,
    w_ref,
    tiles_ref,
    hub_tiles_ref,
    cot_ref,
    out_ref,
    send1_ref,
    send2_ref,
    own_ref,
    features,
    adjoint,
    hub_adjoint,
    grad_w,
    extra,
    sems,
):
    step = pl.program_id(0)
    per_block, blk = tiles_ref.shape[1:3]
    sections = hub_tiles_ref.shape[0]
    width = hub_ref.shape[1]
    own_part = own_ref.shape[0] // blk
    send_part = send1_ref.shape[0]
    own_blocks = x_hbm.shape[0]
    peers = halo1_ref.shape[0]
    height2 = halo2_hbm.shape[1]
    ahead = blk - height2
    odd = halo1_ref.shape[1] - HUBS - ahead
    back1 = send1_ref.shape[1] - EXTRA

    @pl.when(step == 0)
    def _():
        halo = pl.ds(own_blocks, peers)
        copies = [
            pltpu.make_async_copy(x_hbm, features.at[pl.ds(0, own_blocks)], sems.at[0]),
            pltpu.make_async_copy(
                halo2_hbm, features.at[halo, pl.ds(ahead, height2), :], sems.at[1]
            ),
        ]
        for copy in copies:
            copy.start()

        def clear(block, carry):
            adjoint[block] = jnp.zeros((blk, width), F32)
            return carry

        lax.fori_loop(0, adjoint.shape[0], clear, 0, unroll=4)
        hub_adjoint[...] = jnp.zeros_like(hub_adjoint)
        grad_w[...] = jnp.zeros_like(grad_w)
        for copy in copies:
            copy.wait()

        def join(peer, carry):
            place = own_blocks + peer
            features[place, pl.ds(0, ahead), :] = halo1_ref[peer, pl.ds(0, ahead), :]
            late = halo1_ref[peer, pl.ds(ahead, 8), :].astype(F32)
            seam = features[place, pl.ds(ahead, 16), :].astype(F32)
            row = lax.broadcasted_iota(jnp.int32, (8, width), 0)
            head = jnp.where(row < odd, late, seam[:8])
            features[place, pl.ds(ahead, 16), :] = jnp.concatenate([head, seam[8:]]).astype(BF)
            return carry

        lax.fori_loop(0, peers, join, 0, unroll=4)

    @pl.when(step < steps)
    def _():
        weight = w_ref[...]
        weight_twice = jnp.concatenate([weight, weight], axis=0)
        hub_slab = jnp.concatenate([hub_tiles_ref[s] for s in range(sections)], axis=1)
        places = []
        slabs = []
        tiled = []
        for u in range(group):
            first = (step * group + u) * per_block
            places.append([columns_ref[first + t] for t in range(per_block)])
            slabs.append(jnp.concatenate([tiles_ref[u, t] for t in range(per_block)], axis=1))
            blocks = jnp.concatenate([features[place] for place in places[u]], axis=0)
            tiled.append(jnp.dot(slabs[u], blocks, preferred_element_type=F32))
        z = jnp.concatenate(tiled, axis=0)
        z = z + jnp.dot(hub_slab, hub_ref[...], preferred_element_type=F32)
        z_high = z.astype(BF)
        z_low = (z - z_high.astype(F32)).astype(BF)
        preact = jnp.dot(
            jnp.concatenate([z_high, z_low], axis=1), weight_twice, preferred_element_type=F32
        )
        square = preact * preact
        t = jnp.tanh(preact * (GELU_A + (GELU_A * GELU_B) * square))
        half = 0.5 + 0.5 * t
        out_ref[...] = (preact * half).astype(BF)
        slope = half + (0.5 * preact) * (1.0 - t * t) * (GELU_A + (3.0 * GELU_A * GELU_B) * square)
        grad = (cot_ref[...].astype(F32) * slope).astype(BF)
        grad_w[...] += lax.dot_general(
            z_high, grad, (((0,), (0,)), ((), ())), preferred_element_type=F32
        )
        back = lax.dot_general(
            grad, weight, (((1,), (1,)), ((), ())), preferred_element_type=F32
        ).astype(BF)
        back_turned = lax.dot_general(
            weight, grad, (((1,), (1,)), ((), ())), preferred_element_type=F32
        ).astype(BF)
        hub_adjoint[...] += jnp.dot(back_turned, hub_slab, preferred_element_type=F32)
        for u in range(group):
            spread = lax.dot_general(
                slabs[u],
                back[u * blk : (u + 1) * blk],
                (((0,), (0,)), ((), ())),
                preferred_element_type=F32,
            )
            for t in range(per_block):
                adjoint[places[u][t]] += spread[t * blk : (t + 1) * blk]

    @pl.when(step == steps)
    def _():
        for s in range(sections):
            extra[:, s, :] = hub_adjoint[:, s * blk : (s + 1) * blk].T
        total = grad_w[...]
        high = total.astype(BF).astype(F32)
        low = total - high
        pieces = total.shape[1] // width
        for piece in range(pieces):
            part = slice(piece * width, (piece + 1) * width)
            extra[:, sections + piece, :] = high[:, part]
            extra[:, sections + pieces + piece, :] = low[:, part]

    @pl.when(step >= steps)
    def _():
        final = step - steps
        for block in range(own_part):
            own_ref[pl.ds(block * blk, blk), :] = adjoint[final * own_part + block]

        def finish(k, carry):
            peer = final * send_part + k
            rows = adjoint[own_blocks + peer]
            tail = extra[peer]
            send1_ref[k] = jnp.concatenate([rows[:back1], tail], axis=0).astype(BF)
            send2_ref[k] = jnp.concatenate([rows[back1:], tail], axis=0).astype(BF)
            return carry

        lax.fori_loop(0, send_part, finish, 0, unroll=4)


def layer(features, halo1, halo2, hub, weight, tiles, tile_columns, hub_tiles, cotangent):
    blocks, per_block, blk, _ = tiles.shape
    width, width_out = weight.shape
    sections = hub_tiles.shape[0]
    peers = halo1.shape[0]
    rows = blocks * blk
    group = 8
    steps = blocks // group
    finals = 4
    height1 = FIRST_BACK + EXTRA
    height2 = blk - FIRST_BACK + EXTRA

    def work(i):
        return jnp.minimum(i, steps - 1)

    def final(i):
        return jnp.maximum(i - steps, 0)

    return pl.pallas_call(
        functools.partial(layer_kernel, group, steps),
        grid_spec=pltpu.PrefetchScalarGridSpec(
            num_scalar_prefetch=1,
            grid=(steps + finals,),
            in_specs=[
                pl.BlockSpec(memory_space=pl.ANY),
                pl.BlockSpec(halo1.shape, lambda i, *_: (0, 0, 0)),
                pl.BlockSpec(memory_space=pl.ANY),
                pl.BlockSpec((sections * blk, width), lambda i, *_: (0, 0)),
                pl.BlockSpec((width, width_out), lambda i, *_: (0, 0)),
                pl.BlockSpec((group, per_block, blk, blk), lambda i, *_: (work(i), 0, 0, 0)),
                pl.BlockSpec((sections, group * blk, blk), lambda i, *_: (0, work(i), 0)),
                pl.BlockSpec((group * blk, width_out), lambda i, *_: (work(i), 0)),
            ],
            out_specs=[
                pl.BlockSpec((group * blk, width_out), lambda i, *_: (work(i), 0)),
                pl.BlockSpec((peers // finals, height1, width), lambda i, *_: (final(i), 0, 0)),
                pl.BlockSpec((peers // finals, height2, width), lambda i, *_: (final(i), 0, 0)),
                pl.BlockSpec((rows // finals, width), lambda i, *_: (final(i), 0)),
            ],
            scratch_shapes=[
                pltpu.VMEM((blocks + peers, blk, width), BF),
                pltpu.VMEM((blocks + peers, blk, width), F32),
                pltpu.VMEM((width, sections * blk), F32),
                pltpu.VMEM((width, width_out), F32),
                pltpu.VMEM((peers, EXTRA, width), F32),
                pltpu.SemaphoreType.DMA((2,)),
            ],
        ),
        out_shape=[
            jax.ShapeDtypeStruct((rows, width_out), BF),
            jax.ShapeDtypeStruct((peers, height1, width), BF),
            jax.ShapeDtypeStruct((peers, height2, width), BF),
            jax.ShapeDtypeStruct((rows, width), F32),
        ],
        compiler_params=pltpu.CompilerParams(vmem_limit_bytes=LAYER_LIMIT),
    )(
        tile_columns.reshape(-1),
        features.reshape(blocks, blk, width),
        halo1,
        halo2,
        hub,
        weight,
        tiles,
        hub_tiles,
        cotangent,
    )


def add_rows(totals, places, buffer, base):
    sums = [
        totals[v][pl.ds(place + PAD, 1), :] + buffer[pl.ds(base + v, 1), :]
        for v, place in enumerate(places)
    ]
    for v, place in enumerate(places):
        totals[v][pl.ds(place + PAD, 1), :] = sums[v]


def begin_totals(totals, start_ref):
    totals[0][pl.ds(PAD, start_ref.shape[0]), :] = start_ref[...]
    for total in totals[1:]:
        total[...] = jnp.zeros_like(total)


def sum_totals(totals, rows):
    live = pl.ds(PAD, rows)
    t0, t1, t2, t3 = totals
    return (t0[live, :] + t1[live, :]) + (t2[live, :] + t3[live, :])


def scatter_kernel(lists, slots, stop, list_ref, back_ref, start_ref, out_ref, t0, t1, t2, t3, buffer):
    step = pl.program_id(0)
    totals = (t0, t1, t2, t3)
    group = 16

    @pl.when(step == 0)
    def _():
        begin_totals(totals, start_ref)

    def one_list(k, carry):
        start = (step * lists + k) * slots
        buffer[...] = back_ref[k].astype(F32)

        def work(base, end):
            for slot in range(base, end, 4):
                places = [list_ref[start + slot + v] for v in range(4)]
                add_rows(totals, places, buffer, slot)

        work(0, LIVE)
        each_live_group(list_ref, start, LIVE, stop, group, work)
        return carry

    lax.fori_loop(0, lists, one_list, 0)

    @pl.when(step == pl.num_programs(0) - 1)
    def _():
        out_ref[...] = sum_totals(totals, start_ref.shape[0])


def scatter_first(send_lists, returned, start):
    peers, slots = send_lists.shape
    rows, width = start.shape
    lists = 32
    height = returned.shape[1]
    return pl.pallas_call(
        functools.partial(scatter_kernel, lists, slots, height - EXTRA),
        grid_spec=pltpu.PrefetchScalarGridSpec(
            num_scalar_prefetch=1,
            grid=(peers // lists,),
            in_specs=[
                pl.BlockSpec((lists, height, width), lambda i, *_: (i, 0, 0)),
                pl.BlockSpec((rows, width), lambda i, *_: (0, 0)),
            ],
            out_specs=pl.BlockSpec((rows, width), lambda i, *_: (0, 0)),
            scratch_shapes=[pltpu.VMEM((rows + PAD, width), F32)] * 4
            + [pltpu.VMEM((height, width), F32)],
        ),
        out_shape=jax.ShapeDtypeStruct((rows, width), F32),
        compiler_params=pltpu.CompilerParams(vmem_limit_bytes=VMEM_LIMIT),
    )(send_lists.reshape(-1), returned, start)


def last_kernel(
    sections,
    list_ref,
    hub_ref,
    owned_ref,
    back_ref,
    start_ref,
    out_ref,
    grad_w_ref,
    t0,
    t1,
    t2,
    t3,
    buffer,
    grad_w,
):
    totals = (t0, t1, t2, t3)
    peers, height, width = back_ref.shape
    count = height - EXTRA
    group = 16
    pieces = grad_w_ref.shape[1] // width
    begin_totals(totals, start_ref)

    def widen(part, carry):
        for k in range(8):
            peer = part * 8 + k
            buffer[peer] = back_ref[peer].astype(F32)
            for piece in range(pieces):
                high = count + sections + piece
                low = high + pieces
                grad_w[piece, pl.ds(peer, 1), :] = (
                    buffer[peer, high : high + 1, :] + buffer[peer, low : low + 1, :]
                )
        return carry

    lax.fori_loop(0, peers // 8, widen, 0)

    def one_list(peer, carry):
        rows = buffer.at[peer]

        def work(base, end):
            for slot in range(base, end, 4):
                places = [list_ref[peer * count + slot + v] for v in range(4)]
                add_rows(totals, places, rows, slot)

        each_live_group(list_ref, peer * count, 0, count, group, work)
        return carry

    lax.fori_loop(0, peers, one_list, 0, unroll=2)

    for section in range(sections):

        @pl.when(owned_ref[section] != 0)
        def _():
            def some_rows(part, carry):
                for k in range(0, group, 4):
                    for v in range(4):
                        peer = part * group + k + v
                        place = hub_ref[section * peers + peer] + PAD
                        row = buffer[peer, count + section : count + section + 1, :]
                        totals[v][pl.ds(place, 1), :] += row
                return carry

            lax.fori_loop(0, peers // group, some_rows, 0)

    for piece in range(pieces):
        grad_w_ref[:, piece * width : (piece + 1) * width] = grad_w[piece]
    out_ref[...] = sum_totals(totals, start_ref.shape[0]).astype(BF)


def scatter_last(send_lists, hub_rows, owned, returned, start, width_out):
    peers = send_lists.shape[0]
    rows, width = start.shape
    height = returned.shape[1]
    return pl.pallas_call(
        functools.partial(last_kernel, hub_rows.shape[0]),
        grid_spec=pltpu.PrefetchScalarGridSpec(
            num_scalar_prefetch=3,
            grid=(1,),
            in_specs=[
                pl.BlockSpec((peers, height, width), lambda i, *_: (0, 0, 0)),
                pl.BlockSpec((rows, width), lambda i, *_: (0, 0)),
            ],
            out_specs=[
                pl.BlockSpec((rows, width), lambda i, *_: (0, 0)),
                pl.BlockSpec((width, width_out), lambda i, *_: (0, 0)),
            ],
            scratch_shapes=[pltpu.VMEM((rows + PAD, width), F32)] * 4
            + [
                pltpu.VMEM((peers, height, width), F32),
                pltpu.VMEM((width_out // width, peers, width), F32),
            ],
        ),
        out_shape=[
            jax.ShapeDtypeStruct((rows, width), BF),
            jax.ShapeDtypeStruct((width, width_out), F32),
        ],
        compiler_params=pltpu.CompilerParams(vmem_limit_bytes=VMEM_LIMIT),
    )(send_lists.reshape(-1), hub_rows.reshape(-1), owned, returned, start)


def exchange(array):
    return lax.all_to_all(array, "rows", split_axis=0, concat_axis=0, tiled=True)


def body(
    features,
    weight,
    adjacency_tiles,
    tile_columns,
    send_rows,
    hub_owner,
    hub_rows,
    hub_tiles,
    cotangent,
):
    device = lax.axis_index("rows")
    sections, peers = hub_rows.shape
    width, width_out = weight.shape
    pieces = width_out // width
    send_lists = send_rows[0]
    slots = send_lists.shape[1]

    halo1 = exchange(gather_rows(features, send_lists, hub_rows, 0, FIRST_OUT))
    part = gather_rows(features, send_lists, hub_rows, FIRST_OUT, slots)
    hub_mine = halo1[hub_owner, FIRST_OUT + jnp.arange(sections)]
    part = part.at[:, :sections].set(
        jnp.broadcast_to(hub_mine[None], (peers, sections, width))
    )
    halo2 = exchange(part)
    hub = halo2[:, :sections].transpose(1, 0, 2).reshape(sections * peers, width)

    output, send1, send2, own = layer(
        features, halo1, halo2, hub, weight, adjacency_tiles, tile_columns, hub_tiles, cotangent
    )

    back1 = exchange(send1)
    sums = jnp.sum(back1[:, FIRST_BACK:].astype(F32), axis=0)
    weight_row = sums[sections : sections + pieces] + sums[sections + pieces :]
    high = weight_row.astype(BF)
    low = (weight_row - high.astype(F32)).astype(BF)
    mine = jnp.concatenate([sums[:sections].astype(BF), high, low], axis=0)
    end = slots - FIRST_BACK
    send2 = send2.at[:, end:].set(jnp.broadcast_to(mine[None], (peers,) + mine.shape))
    back2 = exchange(send2)

    owned = (hub_owner == device).astype(jnp.int32)
    total = scatter_first(send_lists, back1, own)
    grad_features, grad_weight = scatter_last(
        send_lists[:, FIRST_BACK:], hub_rows, owned, back2, total, width_out
    )
    return (output, grad_features, grad_weight)


def solution(mesh):
    return jax.shard_map(
        body,
        mesh=mesh,
        in_specs=(
            P("rows", None),
            P(),
            P("rows", None, None, None),
            P("rows", None),
            P("rows", None, None),
            P(),
            P(),
            P(None, "rows", None),
            P("rows", None),
        ),
        out_specs=(P("rows", None), P("rows", None), P()),
        check_vma=False,
    )
```

```python
import functools

import jax
import jax.numpy as jnp
from jax import lax
from jax.experimental import pallas as pl
from jax.experimental.pallas import tpu as pltpu
from jax.sharding import PartitionSpec as P

BF = jnp.bfloat16
F32 = jnp.float32
VMEM_LIMIT = 60 * 2**20
LAYER_LIMIT = 50 * 2**20
PAD = 8
EXTRA = 8
HUBS = 4
FIRST_OUT = 36
LIVE = 32
FIRST_BACK = 80
GELU_A = 0.7978845608028654
GELU_B = 0.044715


def each_live_group(list_ref, start, base, stop, group, work):
    if base < stop:
        end = min(stop, (base // group + 1) * group)

        @pl.when(list_ref[start + base] >= 0)
        def _():
            work(base, end)
            each_live_group(list_ref, start, end, stop, group, work)


def gather_kernel(lists, slots, first, stop, list_ref, hub_ref, x_ref, out_ref, wide, buffer):
    step = pl.program_id(0)
    rows = x_ref.shape[0]
    peers = pl.num_programs(0) * lists
    sections = hub_ref.shape[0] // peers
    count = stop - first

    @pl.when(step == 0)
    def _():
        wide[pl.ds(0, PAD), :] = jnp.zeros((PAD, wide.shape[1]), F32)
        wide[pl.ds(PAD, rows), :] = x_ref[...].astype(F32)

    def one_list(k, carry):
        peer = step * lists + k
        start = peer * slots
        if first == 0:
            for slot in range(count):
                row = list_ref[start + slot]
                buffer[slot : slot + 1, :] = wide[pl.ds(row + PAD, 1), :]
            for section in range(sections):
                row = hub_ref[section * peers + peer]
                buffer[count + section : count + section + 1, :] = wide[pl.ds(row + PAD, 1), :]
        else:
            buffer[...] = jnp.zeros_like(buffer)

            def work(base, end):
                for slot in range(base, end):
                    row = list_ref[start + slot]
                    place = HUBS + slot - first
                    buffer[place : place + 1, :] = wide[pl.ds(row + PAD, 1), :]

            each_live_group(list_ref, start, first, stop, 16, work)
        out_ref[k] = buffer[...].astype(BF)
        return carry

    lax.fori_loop(0, lists, one_list, 0, unroll=2 if first == 0 else 1)


def gather_rows(features, send_lists, hub_rows, first, stop):
    peers, slots = send_lists.shape
    rows, width = features.shape
    lists = 32
    height = stop - first + HUBS
    return pl.pallas_call(
        functools.partial(gather_kernel, lists, slots, first, stop),
        grid_spec=pltpu.PrefetchScalarGridSpec(
            num_scalar_prefetch=2,
            grid=(peers // lists,),
            in_specs=[pl.BlockSpec((rows, width), lambda i, *_: (0, 0))],
            out_specs=pl.BlockSpec((lists, height, width), lambda i, *_: (i, 0, 0)),
            scratch_shapes=[
                pltpu.VMEM((rows + PAD, width), F32),
                pltpu.VMEM((height, width), F32),
            ],
        ),
        out_shape=jax.ShapeDtypeStruct((peers, height, width), BF),
        compiler_params=pltpu.CompilerParams(vmem_limit_bytes=VMEM_LIMIT),
    )(send_lists.reshape(-1), hub_rows.reshape(-1), features)


def layer_kernel(
    group,
    steps,
    columns_ref,
    x_hbm,
    halo1_ref,
    halo2_hbm,
    w_ref,
    tiles_ref,
    hub_tiles_ref,
    cot_ref,
    out_ref,
    send_ref,
    back_ref,
    features,
    hub_rows,
    hub,
    adjoint,
    hub_adjoint,
    grad_w,
    extra,
    sems,
):
    step = pl.program_id(0)
    per_block, blk = tiles_ref.shape[1:3]
    sections = hub_tiles_ref.shape[0]
    width = w_ref.shape[0]
    send_part = send_ref.shape[0]
    own_blocks = x_hbm.shape[0]
    peers = halo1_ref.shape[0]
    height2 = halo2_hbm.shape[1]
    ahead = blk - height2
    odd = halo1_ref.shape[1] - HUBS - ahead
    kept = adjoint.shape[1]

    @pl.when(step == 0)
    def _():
        halo = pl.ds(own_blocks, peers)
        copies = [
            pltpu.make_async_copy(x_hbm, features.at[pl.ds(0, own_blocks)], sems.at[0]),
            pltpu.make_async_copy(
                halo2_hbm, features.at[halo, pl.ds(ahead, height2), :], sems.at[1]
            ),
        ]
        for copy in copies:
            copy.start()

        def clear(block, carry):
            adjoint[block] = jnp.zeros((kept, width), F32)
            return carry

        lax.fori_loop(0, adjoint.shape[0], clear, 0, unroll=4)
        hub_adjoint[...] = jnp.zeros_like(hub_adjoint)
        grad_w[...] = jnp.zeros_like(grad_w)
        for copy in copies:
            copy.wait()

        def join(peer, carry):
            place = own_blocks + peer
            features[place, pl.ds(0, ahead), :] = halo1_ref[peer, pl.ds(0, ahead), :]
            late = halo1_ref[peer, pl.ds(ahead, 8), :].astype(F32)
            seam = features[place, pl.ds(ahead, 16), :].astype(F32)
            for section in range(sections):
                hub_rows[section, pl.ds(peer, 1), :] = seam[section : section + 1]
            row = lax.broadcasted_iota(jnp.int32, (8, width), 0)
            head = jnp.where(row < odd, late, seam[:8])
            features[place, pl.ds(ahead, 16), :] = jnp.concatenate([head, seam[8:]]).astype(BF)
            return carry

        lax.fori_loop(0, peers, join, 0, unroll=4)
        for section in range(sections):
            hub[pl.ds(section * blk, blk), :] = hub_rows[section].astype(BF)

    @pl.when(step < steps)
    def _():
        weight = w_ref[...]
        weight_twice = jnp.concatenate([weight, weight], axis=0)
        hub_slab = jnp.concatenate([hub_tiles_ref[s] for s in range(sections)], axis=1)
        places = []
        slabs = []
        tiled = []
        for u in range(group):
            first = (step * group + u) * per_block
            places.append([columns_ref[first + t] for t in range(per_block)])
            slabs.append(jnp.concatenate([tiles_ref[u, t] for t in range(per_block)], axis=1))
            blocks = jnp.concatenate([features[place] for place in places[u]], axis=0)
            tiled.append(jnp.dot(slabs[u], blocks, preferred_element_type=F32))
        z = jnp.concatenate(tiled, axis=0)
        z = z + jnp.dot(hub_slab, hub[...], preferred_element_type=F32)
        z_high = z.astype(BF)
        z_low = (z - z_high.astype(F32)).astype(BF)
        preact = jnp.dot(
            jnp.concatenate([z_high, z_low], axis=1), weight_twice, preferred_element_type=F32
        )
        square = preact * preact
        t = jnp.tanh(preact * (GELU_A + (GELU_A * GELU_B) * square))
        half = 0.5 + 0.5 * t
        out_ref[...] = (preact * half).astype(BF)
        slope = half + (0.5 * preact) * (1.0 - t * t) * (GELU_A + (3.0 * GELU_A * GELU_B) * square)
        grad = (cot_ref[...].astype(F32) * slope).astype(BF)
        grad_w[...] += lax.dot_general(
            z_high, grad, (((0,), (0,)), ((), ())), preferred_element_type=F32
        )
        back = lax.dot_general(
            grad, weight, (((1,), (1,)), ((), ())), preferred_element_type=F32
        ).astype(BF)
        back_ref[...] = back
        back_turned = lax.dot_general(
            weight, grad, (((1,), (1,)), ((), ())), preferred_element_type=F32
        ).astype(BF)
        hub_adjoint[...] += jnp.dot(back_turned, hub_slab, preferred_element_type=F32)
        for u in range(group):
            turned = slabs[u].T
            turned = jnp.concatenate(
                [turned[t * blk : t * blk + kept] for t in range(per_block)], axis=0
            )
            spread = jnp.dot(turned, back[u * blk : (u + 1) * blk], preferred_element_type=F32)
            for t in range(per_block):
                adjoint[places[u][t]] += spread[t * kept : (t + 1) * kept]

    @pl.when(step == steps)
    def _():
        for s in range(sections):
            extra[:, s, :] = hub_adjoint[:, s * blk : (s + 1) * blk].T
        total = grad_w[...]
        high = total.astype(BF).astype(F32)
        low = total - high
        pieces = total.shape[1] // width
        for piece in range(pieces):
            part = slice(piece * width, (piece + 1) * width)
            extra[:, sections + piece, :] = high[:, part]
            extra[:, sections + pieces + piece, :] = low[:, part]

    @pl.when(step >= steps)
    def _():
        final = step - steps

        def finish(k, carry):
            peer = final * send_part + k
            rows = jnp.concatenate([adjoint[own_blocks + peer], extra[peer]], axis=0)
            send_ref[k] = rows.astype(BF)
            return carry

        lax.fori_loop(0, send_part, finish, 0, unroll=4)


def layer(features, halo1, halo2, weight, tiles, tile_columns, hub_tiles, cotangent):
    blocks, per_block, blk, _ = tiles.shape
    width, width_out = weight.shape
    sections = hub_tiles.shape[0]
    peers = halo1.shape[0]
    rows = blocks * blk
    group = 8
    steps = blocks // group
    finals = 4
    height1 = FIRST_BACK + EXTRA

    def work(i):
        return jnp.minimum(i, steps - 1)

    def final(i):
        return jnp.maximum(i - steps, 0)

    return pl.pallas_call(
        functools.partial(layer_kernel, group, steps),
        grid_spec=pltpu.PrefetchScalarGridSpec(
            num_scalar_prefetch=1,
            grid=(steps + finals,),
            in_specs=[
                pl.BlockSpec(memory_space=pl.ANY),
                pl.BlockSpec(halo1.shape, lambda i, *_: (0, 0, 0)),
                pl.BlockSpec(memory_space=pl.ANY),
                pl.BlockSpec((width, width_out), lambda i, *_: (0, 0)),
                pl.BlockSpec((group, per_block, blk, blk), lambda i, *_: (work(i), 0, 0, 0)),
                pl.BlockSpec((sections, group * blk, blk), lambda i, *_: (0, work(i), 0)),
                pl.BlockSpec((group * blk, width_out), lambda i, *_: (work(i), 0)),
            ],
            out_specs=[
                pl.BlockSpec((group * blk, width_out), lambda i, *_: (work(i), 0)),
                pl.BlockSpec((peers // finals, height1, width), lambda i, *_: (final(i), 0, 0)),
                pl.BlockSpec((group * blk, width), lambda i, *_: (work(i), 0)),
            ],
            scratch_shapes=[
                pltpu.VMEM((blocks + peers, blk, width), BF),
                pltpu.VMEM((sections, peers, width), F32),
                pltpu.VMEM((sections * blk, width), BF),
                pltpu.VMEM((blocks + peers, FIRST_BACK, width), F32),
                pltpu.VMEM((width, sections * blk), F32),
                pltpu.VMEM((width, width_out), F32),
                pltpu.VMEM((peers, EXTRA, width), F32),
                pltpu.SemaphoreType.DMA((2,)),
            ],
        ),
        out_shape=[
            jax.ShapeDtypeStruct((rows, width_out), BF),
            jax.ShapeDtypeStruct((peers, height1, width), BF),
            jax.ShapeDtypeStruct((rows, width), BF),
        ],
        compiler_params=pltpu.CompilerParams(vmem_limit_bytes=LAYER_LIMIT),
    )(
        tile_columns.reshape(-1),
        features.reshape(blocks, blk, width),
        halo1,
        halo2,
        weight,
        tiles,
        hub_tiles,
        cotangent,
    )


def rest_kernel(group, steps, columns_ref, back_ref, tiles_ref, send_ref, own_ref, adjoint):
    step = pl.program_id(0)
    per_block, blk = tiles_ref.shape[1:3]
    width = back_ref.shape[1]
    own_part = own_ref.shape[0] // blk
    send_part, height, _ = send_ref.shape
    own_blocks = own_part * (pl.num_programs(0) - steps)

    @pl.when(step == 0)
    def _():
        def clear(block, carry):
            adjoint[block] = jnp.zeros((blk, width), F32)
            return carry

        lax.fori_loop(0, adjoint.shape[0], clear, 0, unroll=4)

    @pl.when(step < steps)
    def _():
        for u in range(group):
            first = (step * group + u) * per_block
            slab = jnp.concatenate([tiles_ref[u, t] for t in range(per_block)], axis=1)
            spread = lax.dot_general(
                slab,
                back_ref[u * blk : (u + 1) * blk, :],
                (((0,), (0,)), ((), ())),
                preferred_element_type=F32,
            )
            for t in range(per_block):
                adjoint[columns_ref[first + t]] += spread[t * blk : (t + 1) * blk]

    @pl.when(step >= steps)
    def _():
        final = step - steps
        for block in range(own_part):
            own_ref[pl.ds(block * blk, blk), :] = adjoint[final * own_part + block]

        def finish(k, carry):
            rows = adjoint[own_blocks + final * send_part + k]
            tail = jnp.zeros((EXTRA, width), F32)
            send_ref[k] = jnp.concatenate([rows[blk + EXTRA - height :], tail], axis=0).astype(BF)
            return carry

        lax.fori_loop(0, send_part, finish, 0, unroll=4)


def rest_of_adjoint(back, tiles, tile_columns, peers):
    blocks, per_block, blk, _ = tiles.shape
    rows, width = back.shape
    group = 8
    steps = blocks // group
    finals = 4
    height = blk - FIRST_BACK + EXTRA

    def work(i):
        return jnp.minimum(i, steps - 1)

    def final(i):
        return jnp.maximum(i - steps, 0)

    return pl.pallas_call(
        functools.partial(rest_kernel, group, steps),
        grid_spec=pltpu.PrefetchScalarGridSpec(
            num_scalar_prefetch=1,
            grid=(steps + finals,),
            in_specs=[
                pl.BlockSpec((group * blk, width), lambda i, *_: (work(i), 0)),
                pl.BlockSpec((group, per_block, blk, blk), lambda i, *_: (work(i), 0, 0, 0)),
            ],
            out_specs=[
                pl.BlockSpec((peers // finals, height, width), lambda i, *_: (final(i), 0, 0)),
                pl.BlockSpec((rows // finals, width), lambda i, *_: (final(i), 0)),
            ],
            scratch_shapes=[pltpu.VMEM((blocks + peers, blk, width), F32)],
        ),
        out_shape=[
            jax.ShapeDtypeStruct((peers, height, width), BF),
            jax.ShapeDtypeStruct((rows, width), F32),
        ],
        compiler_params=pltpu.CompilerParams(vmem_limit_bytes=VMEM_LIMIT),
    )(tile_columns.reshape(-1), back, tiles)


def add_rows(totals, places, buffer, base):
    sums = [
        totals[v][pl.ds(place + PAD, 1), :] + buffer[pl.ds(base + v, 1), :]
        for v, place in enumerate(places)
    ]
    for v, place in enumerate(places):
        totals[v][pl.ds(place + PAD, 1), :] = sums[v]


def begin_totals(totals, start_ref):
    totals[0][pl.ds(PAD, start_ref.shape[0]), :] = start_ref[...]
    for total in totals[1:]:
        total[...] = jnp.zeros_like(total)


def sum_totals(totals, rows):
    live = pl.ds(PAD, rows)
    t0, t1, t2, t3 = totals
    return (t0[live, :] + t1[live, :]) + (t2[live, :] + t3[live, :])


def scatter_kernel(lists, slots, stop, list_ref, back_ref, start_ref, out_ref, t0, t1, t2, t3, buffer):
    step = pl.program_id(0)
    totals = (t0, t1, t2, t3)
    group = 16

    @pl.when(step == 0)
    def _():
        begin_totals(totals, start_ref)

    def one_list(k, carry):
        start = (step * lists + k) * slots
        buffer[...] = back_ref[k].astype(F32)

        def work(base, end):
            for slot in range(base, end, 4):
                places = [list_ref[start + slot + v] for v in range(4)]
                add_rows(totals, places, buffer, slot)

        work(0, LIVE)
        each_live_group(list_ref, start, LIVE, stop, group, work)
        return carry

    lax.fori_loop(0, lists, one_list, 0)

    @pl.when(step == pl.num_programs(0) - 1)
    def _():
        out_ref[...] = sum_totals(totals, start_ref.shape[0])


def scatter_first(send_lists, returned, start):
    peers, slots = send_lists.shape
    rows, width = start.shape
    lists = 32
    height = returned.shape[1]
    return pl.pallas_call(
        functools.partial(scatter_kernel, lists, slots, height - EXTRA),
        grid_spec=pltpu.PrefetchScalarGridSpec(
            num_scalar_prefetch=1,
            grid=(peers // lists,),
            in_specs=[
                pl.BlockSpec((lists, height, width), lambda i, *_: (i, 0, 0)),
                pl.BlockSpec((rows, width), lambda i, *_: (0, 0)),
            ],
            out_specs=pl.BlockSpec((rows, width), lambda i, *_: (0, 0)),
            scratch_shapes=[pltpu.VMEM((rows + PAD, width), F32)] * 4
            + [pltpu.VMEM((height, width), F32)],
        ),
        out_shape=jax.ShapeDtypeStruct((rows, width), F32),
        compiler_params=pltpu.CompilerParams(vmem_limit_bytes=VMEM_LIMIT),
    )(send_lists.reshape(-1), returned, start)


def last_kernel(
    sections,
    list_ref,
    hub_ref,
    owned_ref,
    back_ref,
    start_ref,
    out_ref,
    grad_w_ref,
    t0,
    t1,
    t2,
    t3,
    buffer,
    grad_w,
):
    totals = (t0, t1, t2, t3)
    peers, height, width = back_ref.shape
    count = height - EXTRA
    group = 16
    pieces = grad_w_ref.shape[1] // width
    begin_totals(totals, start_ref)

    def widen(part, carry):
        for k in range(8):
            peer = part * 8 + k
            buffer[peer] = back_ref[peer].astype(F32)
            for piece in range(pieces):
                high = count + sections + piece
                low = high + pieces
                grad_w[piece, pl.ds(peer, 1), :] = (
                    buffer[peer, high : high + 1, :] + buffer[peer, low : low + 1, :]
                )
        return carry

    lax.fori_loop(0, peers // 8, widen, 0)

    def one_list(peer, carry):
        rows = buffer.at[peer]

        def work(base, end):
            for slot in range(base, end, 4):
                places = [list_ref[peer * count + slot + v] for v in range(4)]
                add_rows(totals, places, rows, slot)

        each_live_group(list_ref, peer * count, 0, count, group, work)
        return carry

    lax.fori_loop(0, peers, one_list, 0, unroll=2)

    for section in range(sections):

        @pl.when(owned_ref[section] != 0)
        def _():
            def some_rows(part, carry):
                for k in range(0, group, 4):
                    for v in range(4):
                        peer = part * group + k + v
                        place = hub_ref[section * peers + peer] + PAD
                        row = buffer[peer, count + section : count + section + 1, :]
                        totals[v][pl.ds(place, 1), :] += row
                return carry

            lax.fori_loop(0, peers // group, some_rows, 0)

    for piece in range(pieces):
        grad_w_ref[:, piece * width : (piece + 1) * width] = grad_w[piece]
    out_ref[...] = sum_totals(totals, start_ref.shape[0]).astype(BF)


def scatter_last(send_lists, hub_rows, owned, returned, start, width_out):
    peers = send_lists.shape[0]
    rows, width = start.shape
    height = returned.shape[1]
    return pl.pallas_call(
        functools.partial(last_kernel, hub_rows.shape[0]),
        grid_spec=pltpu.PrefetchScalarGridSpec(
            num_scalar_prefetch=3,
            grid=(1,),
            in_specs=[
                pl.BlockSpec((peers, height, width), lambda i, *_: (0, 0, 0)),
                pl.BlockSpec((rows, width), lambda i, *_: (0, 0)),
            ],
            out_specs=[
                pl.BlockSpec((rows, width), lambda i, *_: (0, 0)),
                pl.BlockSpec((width, width_out), lambda i, *_: (0, 0)),
            ],
            scratch_shapes=[pltpu.VMEM((rows + PAD, width), F32)] * 4
            + [
                pltpu.VMEM((peers, height, width), F32),
                pltpu.VMEM((width_out // width, peers, width), F32),
            ],
        ),
        out_shape=[
            jax.ShapeDtypeStruct((rows, width), BF),
            jax.ShapeDtypeStruct((width, width_out), F32),
        ],
        compiler_params=pltpu.CompilerParams(vmem_limit_bytes=VMEM_LIMIT),
    )(send_lists.reshape(-1), hub_rows.reshape(-1), owned, returned, start)


def exchange(array):
    return lax.all_to_all(array, "rows", split_axis=0, concat_axis=0, tiled=True)


def body(
    features,
    weight,
    adjacency_tiles,
    tile_columns,
    send_rows,
    hub_owner,
    hub_rows,
    hub_tiles,
    cotangent,
):
    device = lax.axis_index("rows")
    sections, peers = hub_rows.shape
    width, width_out = weight.shape
    pieces = width_out // width
    send_lists = send_rows[0]
    slots = send_lists.shape[1]

    halo1 = exchange(gather_rows(features, send_lists, hub_rows, 0, FIRST_OUT))
    part = gather_rows(features, send_lists, hub_rows, FIRST_OUT, slots)
    hub_mine = halo1[hub_owner, FIRST_OUT + jnp.arange(sections)]
    part = part.at[:, :sections].set(
        jnp.broadcast_to(hub_mine[None], (peers, sections, width))
    )
    halo2 = exchange(part)

    output, send1, back = layer(
        features, halo1, halo2, weight, adjacency_tiles, tile_columns, hub_tiles, cotangent
    )

    back1 = exchange(send1)
    send2, own = rest_of_adjoint(back, adjacency_tiles, tile_columns, peers)
    sums = jnp.sum(back1[:, FIRST_BACK:].astype(F32), axis=0)
    weight_row = sums[sections : sections + pieces] + sums[sections + pieces :]
    high = weight_row.astype(BF)
    low = (weight_row - high.astype(F32)).astype(BF)
    mine = jnp.concatenate([sums[:sections].astype(BF), high, low], axis=0)
    end = slots - FIRST_BACK
    send2 = send2.at[:, end:].set(jnp.broadcast_to(mine[None], (peers,) + mine.shape))
    back2 = exchange(send2)

    owned = (hub_owner == device).astype(jnp.int32)
    total = scatter_first(send_lists, back1, own)
    grad_features, grad_weight = scatter_last(
        send_lists[:, FIRST_BACK:], hub_rows, owned, back2, total, width_out
    )
    return (output, grad_features, grad_weight)


def solution(mesh):
    return jax.shard_map(
        body,
        mesh=mesh,
        in_specs=(
            P("rows", None),
            P(),
            P("rows", None, None, None),
            P("rows", None),
            P("rows", None, None),
            P(),
            P(),
            P(None, "rows", None),
            P("rows", None),
        ),
        out_specs=(P("rows", None), P("rows", None), P()),
        check_vma=False,
    )
```

```python
import functools

import jax
import jax.numpy as jnp
from jax import lax
from jax.experimental import pallas as pl
from jax.experimental.pallas import tpu as pltpu
from jax.sharding import PartitionSpec as P

BF = jnp.bfloat16
F32 = jnp.float32
VMEM_LIMIT = 60 * 2**20
LAYER_LIMIT = 50 * 2**20
PAD = 8
EXTRA = 8
HUBS = 4
FIRST_OUT = 36
LIVE = 32
FIRST_BACK = 72
KEPT = 80
GELU_A = 0.7978845608028654
GELU_B = 0.044715


def each_live_group(list_ref, start, base, stop, group, work):
    if base < stop:
        end = min(stop, (base // group + 1) * group)

        @pl.when(list_ref[start + base] >= 0)
        def _():
            work(base, end)
            each_live_group(list_ref, start, end, stop, group, work)


def gather_kernel(lists, slots, first, stop, list_ref, hub_ref, x_ref, out_ref, wide, buffer):
    step = pl.program_id(0)
    rows = x_ref.shape[0]
    peers = pl.num_programs(0) * lists
    sections = hub_ref.shape[0] // peers
    count = stop - first

    @pl.when(step == 0)
    def _():
        wide[pl.ds(0, PAD), :] = jnp.zeros((PAD, wide.shape[1]), F32)
        wide[pl.ds(PAD, rows), :] = x_ref[...].astype(F32)

    height = count + HUBS
    pair = 2

    def one_pair(k, carry):
        for half in range(pair):
            peer = step * lists + k * pair + half
            start = peer * slots
            top = half * height
            if first == 0:
                for slot in range(count):
                    row = list_ref[start + slot]
                    buffer[top + slot : top + slot + 1, :] = wide[pl.ds(row + PAD, 1), :]
                for section in range(sections):
                    row = hub_ref[section * peers + peer]
                    place = top + count + section
                    buffer[place : place + 1, :] = wide[pl.ds(row + PAD, 1), :]
            else:
                buffer[top : top + height, :] = jnp.zeros((height, wide.shape[1]), F32)

                def work(base, end):
                    for slot in range(base, end):
                        row = list_ref[start + slot]
                        place = top + HUBS + slot - first
                        buffer[place : place + 1, :] = wide[pl.ds(row + PAD, 1), :]

                each_live_group(list_ref, start, first, stop, 16, work)
        rows = pair * height
        out_ref[pl.ds(pl.multiple_of(k * rows, rows), rows), :] = buffer[...].astype(BF)
        return carry

    lax.fori_loop(0, lists // pair, one_pair, 0)


def gather_rows(features, send_lists, hub_rows, first, stop):
    peers, slots = send_lists.shape
    rows, width = features.shape
    lists = 32
    height = stop - first + HUBS
    return pl.pallas_call(
        functools.partial(gather_kernel, lists, slots, first, stop),
        grid_spec=pltpu.PrefetchScalarGridSpec(
            num_scalar_prefetch=2,
            grid=(peers // lists,),
            in_specs=[pl.BlockSpec((rows, width), lambda i, *_: (0, 0))],
            out_specs=pl.BlockSpec((lists * height, width), lambda i, *_: (i, 0)),
            scratch_shapes=[
                pltpu.VMEM((rows + PAD, width), F32),
                pltpu.VMEM((2 * height, width), F32),
            ],
        ),
        out_shape=jax.ShapeDtypeStruct((peers * height, width), BF),
        compiler_params=pltpu.CompilerParams(vmem_limit_bytes=VMEM_LIMIT),
    )(send_lists.reshape(-1), hub_rows.reshape(-1), features).reshape(peers, height, width)


def layer_kernel(
    group,
    steps,
    columns_ref,
    x_hbm,
    halo1_ref,
    halo2_hbm,
    w_ref,
    tiles_ref,
    hub_tiles_ref,
    cot_ref,
    out_ref,
    send_ref,
    back_ref,
    features,
    hub_rows,
    hub,
    adjoint,
    hub_adjoint,
    grad_w,
    extra,
    sems,
):
    step = pl.program_id(0)
    per_block, blk = tiles_ref.shape[1:3]
    sections = hub_tiles_ref.shape[0]
    width = w_ref.shape[0]
    send_part = send_ref.shape[0]
    own_blocks = x_hbm.shape[0]
    peers, height2, _ = halo2_hbm.shape
    height1 = halo1_ref.shape[0] // peers
    ahead = blk - height2
    odd = height1 - HUBS - ahead
    kept = adjoint.shape[1]

    @pl.when(step == 0)
    def _():
        halo = pl.ds(own_blocks, peers)
        copies = [
            pltpu.make_async_copy(x_hbm, features.at[pl.ds(0, own_blocks)], sems.at[0]),
            pltpu.make_async_copy(
                halo2_hbm, features.at[halo, pl.ds(ahead, height2), :], sems.at[1]
            ),
        ]
        for copy in copies:
            copy.start()

        def clear(block, carry):
            adjoint[block] = jnp.zeros((kept, width), F32)
            return carry

        lax.fori_loop(0, adjoint.shape[0], clear, 0, unroll=4)
        hub_adjoint[...] = jnp.zeros_like(hub_adjoint)
        grad_w[...] = jnp.zeros_like(grad_w)
        for copy in copies:
            copy.wait()

        def join(k, carry):
            rows = 2 * height1
            part1 = halo1_ref[pl.ds(pl.multiple_of(k * rows, rows), rows), :].astype(F32)
            for half in range(2):
                peer = 2 * k + half
                place = own_blocks + peer
                top = half * height1
                features[place, pl.ds(0, ahead), :] = part1[top : top + ahead].astype(BF)
                late = part1[top + ahead : top + ahead + 8]
                seam = features[place, pl.ds(ahead, 16), :].astype(F32)
                for section in range(sections):
                    hub_rows[section, pl.ds(peer, 1), :] = seam[section : section + 1]
                row = lax.broadcasted_iota(jnp.int32, (8, width), 0)
                head = jnp.where(row < odd, late, seam[:8])
                whole = jnp.concatenate([head, seam[8:]])
                features[place, pl.ds(ahead, 16), :] = whole.astype(BF)
            return carry

        lax.fori_loop(0, peers // 2, join, 0, unroll=2)
        for section in range(sections):
            hub[pl.ds(section * blk, blk), :] = hub_rows[section].astype(BF)

    @pl.when(step < steps)
    def _():
        weight = w_ref[...]
        weight_twice = jnp.concatenate([weight, weight], axis=0)
        hub_slab = jnp.concatenate([hub_tiles_ref[s] for s in range(sections)], axis=1)
        places = []
        slabs = []
        tiled = []
        for u in range(group):
            first = (step * group + u) * per_block
            places.append([columns_ref[first + t] for t in range(per_block)])
            slabs.append(jnp.concatenate([tiles_ref[u, t] for t in range(per_block)], axis=1))
            blocks = jnp.concatenate([features[place] for place in places[u]], axis=0)
            tiled.append(jnp.dot(slabs[u], blocks, preferred_element_type=F32))
        z = jnp.concatenate(tiled, axis=0)
        z = z + jnp.dot(hub_slab, hub[...], preferred_element_type=F32)
        z_high = z.astype(BF)
        z_low = (z - z_high.astype(F32)).astype(BF)
        preact = jnp.dot(
            jnp.concatenate([z_high, z_low], axis=1), weight_twice, preferred_element_type=F32
        )
        square = preact * preact
        t = jnp.tanh(preact * (GELU_A + (GELU_A * GELU_B) * square))
        half = 0.5 + 0.5 * t
        out_ref[...] = (preact * half).astype(BF)
        slope = half + (0.5 * preact) * (1.0 - t * t) * (GELU_A + (3.0 * GELU_A * GELU_B) * square)
        grad = (cot_ref[...].astype(F32) * slope).astype(BF)
        grad_w[...] += lax.dot_general(
            z_high, grad, (((0,), (0,)), ((), ())), preferred_element_type=F32
        )
        back = lax.dot_general(
            grad, weight, (((1,), (1,)), ((), ())), preferred_element_type=F32
        ).astype(BF)
        back_ref[...] = back
        back_turned = lax.dot_general(
            weight, grad, (((1,), (1,)), ((), ())), preferred_element_type=F32
        ).astype(BF)
        hub_adjoint[...] += jnp.dot(back_turned, hub_slab, preferred_element_type=F32)
        for u in range(group):
            turned = slabs[u].T
            turned = jnp.concatenate(
                [turned[t * blk : t * blk + kept] for t in range(per_block)], axis=0
            )
            spread = jnp.dot(turned, back[u * blk : (u + 1) * blk], preferred_element_type=F32)
            for t in range(per_block):
                adjoint[places[u][t]] += spread[t * kept : (t + 1) * kept]

    @pl.when(step == steps)
    def _():
        for s in range(sections):
            extra[:, s, :] = hub_adjoint[:, s * blk : (s + 1) * blk].T
        total = grad_w[...]
        high = total.astype(BF).astype(F32)
        low = total - high
        pieces = total.shape[1] // width
        for piece in range(pieces):
            part = slice(piece * width, (piece + 1) * width)
            extra[:, sections + piece, :] = high[:, part]
            extra[:, sections + pieces + piece, :] = low[:, part]

    @pl.when(step >= steps)
    def _():
        final = step - steps

        def finish(k, carry):
            peer = final * send_part + k
            rows = adjoint[own_blocks + peer][: send_ref.shape[1] - EXTRA]
            send_ref[k] = jnp.concatenate([rows, extra[peer]], axis=0).astype(BF)
            return carry

        lax.fori_loop(0, send_part, finish, 0, unroll=4)


def layer(features, halo1, halo2, weight, tiles, tile_columns, hub_tiles, cotangent):
    blocks, per_block, blk, _ = tiles.shape
    width, width_out = weight.shape
    sections = hub_tiles.shape[0]
    peers = halo1.shape[0]
    rows = blocks * blk
    group = 8
    steps = blocks // group
    finals = 4
    height1 = FIRST_BACK + EXTRA

    def work(i):
        return jnp.minimum(i, steps - 1)

    def final(i):
        return jnp.maximum(i - steps, 0)

    return pl.pallas_call(
        functools.partial(layer_kernel, group, steps),
        grid_spec=pltpu.PrefetchScalarGridSpec(
            num_scalar_prefetch=1,
            grid=(steps + finals,),
            in_specs=[
                pl.BlockSpec(memory_space=pl.ANY),
                pl.BlockSpec((peers * halo1.shape[1], width), lambda i, *_: (0, 0)),
                pl.BlockSpec(memory_space=pl.ANY),
                pl.BlockSpec((width, width_out), lambda i, *_: (0, 0)),
                pl.BlockSpec((group, per_block, blk, blk), lambda i, *_: (work(i), 0, 0, 0)),
                pl.BlockSpec((sections, group * blk, blk), lambda i, *_: (0, work(i), 0)),
                pl.BlockSpec((group * blk, width_out), lambda i, *_: (work(i), 0)),
            ],
            out_specs=[
                pl.BlockSpec((group * blk, width_out), lambda i, *_: (work(i), 0)),
                pl.BlockSpec((peers // finals, height1, width), lambda i, *_: (final(i), 0, 0)),
                pl.BlockSpec((group * blk, width), lambda i, *_: (work(i), 0)),
            ],
            scratch_shapes=[
                pltpu.VMEM((blocks + peers, blk, width), BF),
                pltpu.VMEM((sections, peers, width), F32),
                pltpu.VMEM((sections * blk, width), BF),
                pltpu.VMEM((blocks + peers, KEPT, width), F32),
                pltpu.VMEM((width, sections * blk), F32),
                pltpu.VMEM((width, width_out), F32),
                pltpu.VMEM((peers, EXTRA, width), F32),
                pltpu.SemaphoreType.DMA((2,)),
            ],
        ),
        out_shape=[
            jax.ShapeDtypeStruct((rows, width_out), BF),
            jax.ShapeDtypeStruct((peers, height1, width), BF),
            jax.ShapeDtypeStruct((rows, width), BF),
        ],
        compiler_params=pltpu.CompilerParams(vmem_limit_bytes=LAYER_LIMIT),
    )(
        tile_columns.reshape(-1),
        features.reshape(blocks, blk, width),
        halo1.reshape(-1, width),
        halo2,
        weight,
        tiles,
        hub_tiles,
        cotangent,
    )


def rest_kernel(group, steps, columns_ref, back_ref, tiles_ref, send_ref, own_ref, adjoint):
    step = pl.program_id(0)
    per_block, blk = tiles_ref.shape[1:3]
    width = back_ref.shape[1]
    own_part = own_ref.shape[0] // blk
    send_part, height, _ = send_ref.shape
    own_blocks = own_part * (pl.num_programs(0) - steps)

    @pl.when(step == 0)
    def _():
        def clear(block, carry):
            adjoint[block] = jnp.zeros((blk, width), F32)
            return carry

        lax.fori_loop(0, adjoint.shape[0], clear, 0, unroll=4)

    @pl.when(step < steps)
    def _():
        for u in range(group):
            first = (step * group + u) * per_block
            slab = jnp.concatenate([tiles_ref[u, t] for t in range(per_block)], axis=1)
            spread = lax.dot_general(
                slab,
                back_ref[u * blk : (u + 1) * blk, :],
                (((0,), (0,)), ((), ())),
                preferred_element_type=F32,
            )
            for t in range(per_block):
                adjoint[columns_ref[first + t]] += spread[t * blk : (t + 1) * blk]

    @pl.when(step >= steps)
    def _():
        final = step - steps
        for block in range(own_part):
            own_ref[pl.ds(block * blk, blk), :] = adjoint[final * own_part + block]

        def finish(k, carry):
            rows = adjoint[own_blocks + final * send_part + k]
            tail = jnp.zeros((EXTRA, width), F32)
            send_ref[k] = jnp.concatenate([rows[blk + EXTRA - height :], tail], axis=0).astype(BF)
            return carry

        lax.fori_loop(0, send_part, finish, 0, unroll=4)


def rest_of_adjoint(back, tiles, tile_columns, peers):
    blocks, per_block, blk, _ = tiles.shape
    rows, width = back.shape
    group = 8
    steps = blocks // group
    finals = 4
    height = blk - FIRST_BACK + EXTRA

    def work(i):
        return jnp.minimum(i, steps - 1)

    def final(i):
        return jnp.maximum(i - steps, 0)

    return pl.pallas_call(
        functools.partial(rest_kernel, group, steps),
        grid_spec=pltpu.PrefetchScalarGridSpec(
            num_scalar_prefetch=1,
            grid=(steps + finals,),
            in_specs=[
                pl.BlockSpec((group * blk, width), lambda i, *_: (work(i), 0)),
                pl.BlockSpec((group, per_block, blk, blk), lambda i, *_: (work(i), 0, 0, 0)),
            ],
            out_specs=[
                pl.BlockSpec((peers // finals, height, width), lambda i, *_: (final(i), 0, 0)),
                pl.BlockSpec((rows // finals, width), lambda i, *_: (final(i), 0)),
            ],
            scratch_shapes=[pltpu.VMEM((blocks + peers, blk, width), F32)],
        ),
        out_shape=[
            jax.ShapeDtypeStruct((peers, height, width), BF),
            jax.ShapeDtypeStruct((rows, width), F32),
        ],
        compiler_params=pltpu.CompilerParams(vmem_limit_bytes=VMEM_LIMIT),
    )(tile_columns.reshape(-1), back, tiles)


def add_rows(totals, places, buffer, base):
    sums = [
        totals[v][pl.ds(place + PAD, 1), :] + buffer[pl.ds(base + v, 1), :]
        for v, place in enumerate(places)
    ]
    for v, place in enumerate(places):
        totals[v][pl.ds(place + PAD, 1), :] = sums[v]


def begin_totals(totals, start_ref):
    totals[0][pl.ds(PAD, start_ref.shape[0]), :] = start_ref[...]
    for total in totals[1:]:
        total[...] = jnp.zeros_like(total)


def sum_totals(totals, rows):
    live = pl.ds(PAD, rows)
    t0, t1, t2, t3 = totals
    return (t0[live, :] + t1[live, :]) + (t2[live, :] + t3[live, :])


def scatter_kernel(lists, slots, stop, list_ref, back_ref, start_ref, out_ref, t0, t1, t2, t3, buffer):
    step = pl.program_id(0)
    totals = (t0, t1, t2, t3)
    group = 16

    @pl.when(step == 0)
    def _():
        begin_totals(totals, start_ref)

    def one_list(k, carry):
        start = (step * lists + k) * slots
        buffer[...] = back_ref[k].astype(F32)

        def work(base, end):
            for slot in range(base, end, 4):
                places = [list_ref[start + slot + v] for v in range(4)]
                add_rows(totals, places, buffer, slot)

        work(0, LIVE)
        each_live_group(list_ref, start, LIVE, stop, group, work)
        return carry

    lax.fori_loop(0, lists, one_list, 0)

    @pl.when(step == pl.num_programs(0) - 1)
    def _():
        out_ref[...] = sum_totals(totals, start_ref.shape[0])


def scatter_first(send_lists, returned, start):
    peers, slots = send_lists.shape
    rows, width = start.shape
    lists = 32
    height = returned.shape[1]
    return pl.pallas_call(
        functools.partial(scatter_kernel, lists, slots, height - EXTRA),
        grid_spec=pltpu.PrefetchScalarGridSpec(
            num_scalar_prefetch=1,
            grid=(peers // lists,),
            in_specs=[
                pl.BlockSpec((lists, height, width), lambda i, *_: (i, 0, 0)),
                pl.BlockSpec((rows, width), lambda i, *_: (0, 0)),
            ],
            out_specs=pl.BlockSpec((rows, width), lambda i, *_: (0, 0)),
            scratch_shapes=[pltpu.VMEM((rows + PAD, width), F32)] * 4
            + [pltpu.VMEM((height, width), F32)],
        ),
        out_shape=jax.ShapeDtypeStruct((rows, width), F32),
        compiler_params=pltpu.CompilerParams(vmem_limit_bytes=VMEM_LIMIT),
    )(send_lists.reshape(-1), returned, start)


def last_kernel(
    sections,
    list_ref,
    hub_ref,
    owned_ref,
    back_ref,
    start_ref,
    out_ref,
    grad_w_ref,
    t0,
    t1,
    t2,
    t3,
    buffer,
    grad_w,
):
    totals = (t0, t1, t2, t3)
    peers, height, width = back_ref.shape
    count = height - EXTRA
    group = 16
    pieces = grad_w_ref.shape[1] // width
    begin_totals(totals, start_ref)

    def widen(part, carry):
        for k in range(8):
            peer = part * 8 + k
            buffer[peer] = back_ref[peer].astype(F32)
            for piece in range(pieces):
                high = count + sections + piece
                low = high + pieces
                grad_w[piece, pl.ds(peer, 1), :] = (
                    buffer[peer, high : high + 1, :] + buffer[peer, low : low + 1, :]
                )
        return carry

    lax.fori_loop(0, peers // 8, widen, 0)

    def one_list(peer, carry):
        rows = buffer.at[peer]

        def work(base, end):
            for slot in range(base, end, 4):
                places = [list_ref[peer * count + slot + v] for v in range(4)]
                add_rows(totals, places, rows, slot)

        each_live_group(list_ref, peer * count, 0, count, group, work)
        return carry

    lax.fori_loop(0, peers, one_list, 0, unroll=2)

    for section in range(sections):

        @pl.when(owned_ref[section] != 0)
        def _():
            def some_rows(part, carry):
                for k in range(0, group, 4):
                    for v in range(4):
                        peer = part * group + k + v
                        place = hub_ref[section * peers + peer] + PAD
                        row = buffer[peer, count + section : count + section + 1, :]
                        totals[v][pl.ds(place, 1), :] += row
                return carry

            lax.fori_loop(0, peers // group, some_rows, 0)

    for piece in range(pieces):
        grad_w_ref[:, piece * width : (piece + 1) * width] = grad_w[piece]
    out_ref[...] = sum_totals(totals, start_ref.shape[0]).astype(BF)


def scatter_last(send_lists, hub_rows, owned, returned, start, width_out):
    peers = send_lists.shape[0]
    rows, width = start.shape
    height = returned.shape[1]
    return pl.pallas_call(
        functools.partial(last_kernel, hub_rows.shape[0]),
        grid_spec=pltpu.PrefetchScalarGridSpec(
            num_scalar_prefetch=3,
            grid=(1,),
            in_specs=[
                pl.BlockSpec((peers, height, width), lambda i, *_: (0, 0, 0)),
                pl.BlockSpec((rows, width), lambda i, *_: (0, 0)),
            ],
            out_specs=[
                pl.BlockSpec((rows, width), lambda i, *_: (0, 0)),
                pl.BlockSpec((width, width_out), lambda i, *_: (0, 0)),
            ],
            scratch_shapes=[pltpu.VMEM((rows + PAD, width), F32)] * 4
            + [
                pltpu.VMEM((peers, height, width), F32),
                pltpu.VMEM((width_out // width, peers, width), F32),
            ],
        ),
        out_shape=[
            jax.ShapeDtypeStruct((rows, width), BF),
            jax.ShapeDtypeStruct((width, width_out), F32),
        ],
        compiler_params=pltpu.CompilerParams(vmem_limit_bytes=VMEM_LIMIT),
    )(send_lists.reshape(-1), hub_rows.reshape(-1), owned, returned, start)


def exchange(array):
    return lax.all_to_all(array, "rows", split_axis=0, concat_axis=0, tiled=True)


def body(
    features,
    weight,
    adjacency_tiles,
    tile_columns,
    send_rows,
    hub_owner,
    hub_rows,
    hub_tiles,
    cotangent,
):
    device = lax.axis_index("rows")
    sections, peers = hub_rows.shape
    width, width_out = weight.shape
    pieces = width_out // width
    send_lists = send_rows[0]
    slots = send_lists.shape[1]

    halo1 = exchange(gather_rows(features, send_lists, hub_rows, 0, FIRST_OUT))
    part = gather_rows(features, send_lists, hub_rows, FIRST_OUT, slots)
    hub_mine = halo1[hub_owner, FIRST_OUT + jnp.arange(sections)]
    part = part.at[:, :sections].set(
        jnp.broadcast_to(hub_mine[None], (peers, sections, width))
    )
    halo2 = exchange(part)

    output, send1, back = layer(
        features, halo1, halo2, weight, adjacency_tiles, tile_columns, hub_tiles, cotangent
    )

    back1 = exchange(send1)
    send2, own = rest_of_adjoint(back, adjacency_tiles, tile_columns, peers)
    sums = jnp.sum(back1[:, FIRST_BACK:].astype(F32), axis=0)
    weight_row = sums[sections : sections + pieces] + sums[sections + pieces :]
    high = weight_row.astype(BF)
    low = (weight_row - high.astype(F32)).astype(BF)
    mine = jnp.concatenate([sums[:sections].astype(BF), high, low], axis=0)
    end = slots - FIRST_BACK
    send2 = send2.at[:, end:].set(jnp.broadcast_to(mine[None], (peers,) + mine.shape))
    back2 = exchange(send2)

    owned = (hub_owner == device).astype(jnp.int32)
    total = scatter_first(send_lists, back1, own)
    grad_features, grad_weight = scatter_last(
        send_lists[:, FIRST_BACK:], hub_rows, owned, back2, total, width_out
    )
    return (output, grad_features, grad_weight)


def solution(mesh):
    return jax.shard_map(
        body,
        mesh=mesh,
        in_specs=(
            P("rows", None),
            P(),
            P("rows", None, None, None),
            P("rows", None),
            P("rows", None, None),
            P(),
            P(),
            P(None, "rows", None),
            P("rows", None),
        ),
        out_specs=(P("rows", None), P("rows", None), P()),
        check_vma=False,
    )
```

```python
import functools

import jax
import jax.numpy as jnp
from jax import lax
from jax.experimental import pallas as pl
from jax.experimental.pallas import tpu as pltpu
from jax.sharding import PartitionSpec as P

BF = jnp.bfloat16
F32 = jnp.float32
VMEM_LIMIT = 60 * 2**20
LAYER_LIMIT = 50 * 2**20
PAD = 8
EXTRA = 8
HUBS = 4
FIRST_OUT = 36
LIVE = 32
FIRST_BACK = 88
KEPT = 96
GELU_A = 0.7978845608028654
GELU_B = 0.044715


def each_live_group(list_ref, start, base, stop, group, work):
    if base < stop:
        end = min(stop, (base // group + 1) * group)

        @pl.when(list_ref[start + base] >= 0)
        def _():
            work(base, end)
            each_live_group(list_ref, start, end, stop, group, work)


def gather_kernel(lists, slots, first, stop, list_ref, hub_ref, x_ref, out_ref, wide, buffer):
    step = pl.program_id(0)
    rows = x_ref.shape[0]
    peers = pl.num_programs(0) * lists
    sections = hub_ref.shape[0] // peers
    count = stop - first

    @pl.when(step == 0)
    def _():
        wide[pl.ds(0, PAD), :] = jnp.zeros((PAD, wide.shape[1]), F32)
        wide[pl.ds(PAD, rows), :] = x_ref[...].astype(F32)

    height = count + HUBS
    pair = 2

    def one_pair(k, carry):
        for half in range(pair):
            peer = step * lists + k * pair + half
            start = peer * slots
            top = half * height
            if first == 0:
                for slot in range(count):
                    row = list_ref[start + slot]
                    buffer[top + slot : top + slot + 1, :] = wide[pl.ds(row + PAD, 1), :]
                for section in range(sections):
                    row = hub_ref[section * peers + peer]
                    place = top + count + section
                    buffer[place : place + 1, :] = wide[pl.ds(row + PAD, 1), :]
            else:
                buffer[top : top + height, :] = jnp.zeros((height, wide.shape[1]), F32)

                def work(base, end):
                    for slot in range(base, end):
                        row = list_ref[start + slot]
                        place = top + HUBS + slot - first
                        buffer[place : place + 1, :] = wide[pl.ds(row + PAD, 1), :]

                each_live_group(list_ref, start, first, stop, 16, work)
        rows = pair * height
        out_ref[pl.ds(pl.multiple_of(k * rows, rows), rows), :] = buffer[...].astype(BF)
        return carry

    lax.fori_loop(0, lists // pair, one_pair, 0)


def gather_rows(features, send_lists, hub_rows, first, stop):
    peers, slots = send_lists.shape
    rows, width = features.shape
    lists = 32
    height = stop - first + HUBS
    return pl.pallas_call(
        functools.partial(gather_kernel, lists, slots, first, stop),
        grid_spec=pltpu.PrefetchScalarGridSpec(
            num_scalar_prefetch=2,
            grid=(peers // lists,),
            in_specs=[pl.BlockSpec((rows, width), lambda i, *_: (0, 0))],
            out_specs=pl.BlockSpec((lists * height, width), lambda i, *_: (i, 0)),
            scratch_shapes=[
                pltpu.VMEM((rows + PAD, width), F32),
                pltpu.VMEM((2 * height, width), F32),
            ],
        ),
        out_shape=jax.ShapeDtypeStruct((peers * height, width), BF),
        compiler_params=pltpu.CompilerParams(vmem_limit_bytes=VMEM_LIMIT),
    )(send_lists.reshape(-1), hub_rows.reshape(-1), features).reshape(peers, height, width)


def layer_kernel(
    group,
    steps,
    columns_ref,
    x_hbm,
    halo1_ref,
    halo2_hbm,
    w_ref,
    tiles_ref,
    hub_tiles_ref,
    cot_ref,
    out_ref,
    send_ref,
    back_ref,
    features,
    hub_rows,
    hub,
    adjoint,
    hub_adjoint,
    grad_w,
    extra,
    sems,
):
    step = pl.program_id(0)
    per_block, blk = tiles_ref.shape[1:3]
    sections = hub_tiles_ref.shape[0]
    width = w_ref.shape[0]
    send_part = send_ref.shape[0]
    own_blocks = x_hbm.shape[0]
    peers, height2, _ = halo2_hbm.shape
    height1 = halo1_ref.shape[0] // peers
    ahead = blk - height2
    odd = height1 - HUBS - ahead
    kept = adjoint.shape[1]

    @pl.when(step == 0)
    def _():
        halo = pl.ds(own_blocks, peers)
        copies = [
            pltpu.make_async_copy(x_hbm, features.at[pl.ds(0, own_blocks)], sems.at[0]),
            pltpu.make_async_copy(
                halo2_hbm, features.at[halo, pl.ds(ahead, height2), :], sems.at[1]
            ),
        ]
        for copy in copies:
            copy.start()

        def clear(block, carry):
            adjoint[block] = jnp.zeros((kept, width), F32)
            return carry

        lax.fori_loop(0, adjoint.shape[0], clear, 0, unroll=4)
        hub_adjoint[...] = jnp.zeros_like(hub_adjoint)
        grad_w[...] = jnp.zeros_like(grad_w)
        for copy in copies:
            copy.wait()

        def join(k, carry):
            rows = 2 * height1
            part1 = halo1_ref[pl.ds(pl.multiple_of(k * rows, rows), rows), :].astype(F32)
            for half in range(2):
                peer = 2 * k + half
                place = own_blocks + peer
                top = half * height1
                features[place, pl.ds(0, ahead), :] = part1[top : top + ahead].astype(BF)
                late = part1[top + ahead : top + ahead + 8]
                seam = features[place, pl.ds(ahead, 16), :].astype(F32)
                for section in range(sections):
                    hub_rows[section, pl.ds(peer, 1), :] = seam[section : section + 1]
                row = lax.broadcasted_iota(jnp.int32, (8, width), 0)
                head = jnp.where(row < odd, late, seam[:8])
                whole = jnp.concatenate([head, seam[8:]])
                features[place, pl.ds(ahead, 16), :] = whole.astype(BF)
            return carry

        lax.fori_loop(0, peers // 2, join, 0, unroll=2)
        for section in range(sections):
            hub[pl.ds(section * blk, blk), :] = hub_rows[section].astype(BF)

    @pl.when(step < steps)
    def _():
        weight = w_ref[...]
        weight_twice = jnp.concatenate([weight, weight], axis=0)
        hub_slab = jnp.concatenate([hub_tiles_ref[s] for s in range(sections)], axis=1)
        places = []
        slabs = []
        tiled = []
        for u in range(group):
            first = (step * group + u) * per_block
            places.append([columns_ref[first + t] for t in range(per_block)])
            slabs.append(jnp.concatenate([tiles_ref[u, t] for t in range(per_block)], axis=1))
            blocks = jnp.concatenate([features[place] for place in places[u]], axis=0)
            tiled.append(jnp.dot(slabs[u], blocks, preferred_element_type=F32))
        z = jnp.concatenate(tiled, axis=0)
        z = z + jnp.dot(hub_slab, hub[...], preferred_element_type=F32)
        z_high = z.astype(BF)
        z_low = (z - z_high.astype(F32)).astype(BF)
        preact = jnp.dot(
            jnp.concatenate([z_high, z_low], axis=1), weight_twice, preferred_element_type=F32
        )
        square = preact * preact
        t = jnp.tanh(preact * (GELU_A + (GELU_A * GELU_B) * square))
        half = 0.5 + 0.5 * t
        out_ref[...] = (preact * half).astype(BF)
        slope = half + (0.5 * preact) * (1.0 - t * t) * (GELU_A + (3.0 * GELU_A * GELU_B) * square)
        grad = (cot_ref[...].astype(F32) * slope).astype(BF)
        grad_w[...] += lax.dot_general(
            z_high, grad, (((0,), (0,)), ((), ())), preferred_element_type=F32
        )
        back = lax.dot_general(
            grad, weight, (((1,), (1,)), ((), ())), preferred_element_type=F32
        ).astype(BF)
        back_ref[...] = back
        back_turned = lax.dot_general(
            weight, grad, (((1,), (1,)), ((), ())), preferred_element_type=F32
        ).astype(BF)
        hub_adjoint[...] += jnp.dot(back_turned, hub_slab, preferred_element_type=F32)
        for u in range(group):
            turned = slabs[u].T
            turned = jnp.concatenate(
                [turned[t * blk : t * blk + kept] for t in range(per_block)], axis=0
            )
            spread = jnp.dot(turned, back[u * blk : (u + 1) * blk], preferred_element_type=F32)
            for t in range(per_block):
                adjoint[places[u][t]] += spread[t * kept : (t + 1) * kept]

    @pl.when(step == steps)
    def _():
        for s in range(sections):
            extra[:, s, :] = hub_adjoint[:, s * blk : (s + 1) * blk].T
        total = grad_w[...]
        high = total.astype(BF).astype(F32)
        low = total - high
        pieces = total.shape[1] // width
        for piece in range(pieces):
            part = slice(piece * width, (piece + 1) * width)
            extra[:, sections + piece, :] = high[:, part]
            extra[:, sections + pieces + piece, :] = low[:, part]

    @pl.when(step >= steps)
    def _():
        final = step - steps

        def finish(k, carry):
            peer = final * send_part + k
            rows = adjoint[own_blocks + peer][: send_ref.shape[1] - EXTRA]
            send_ref[k] = jnp.concatenate([rows, extra[peer]], axis=0).astype(BF)
            return carry

        lax.fori_loop(0, send_part, finish, 0, unroll=4)


def layer(features, halo1, halo2, weight, tiles, tile_columns, hub_tiles, cotangent):
    blocks, per_block, blk, _ = tiles.shape
    width, width_out = weight.shape
    sections = hub_tiles.shape[0]
    peers = halo1.shape[0]
    rows = blocks * blk
    group = 8
    steps = blocks // group
    finals = 4
    height1 = FIRST_BACK + EXTRA

    def work(i):
        return jnp.minimum(i, steps - 1)

    def final(i):
        return jnp.maximum(i - steps, 0)

    return pl.pallas_call(
        functools.partial(layer_kernel, group, steps),
        grid_spec=pltpu.PrefetchScalarGridSpec(
            num_scalar_prefetch=1,
            grid=(steps + finals,),
            in_specs=[
                pl.BlockSpec(memory_space=pl.ANY),
                pl.BlockSpec((peers * halo1.shape[1], width), lambda i, *_: (0, 0)),
                pl.BlockSpec(memory_space=pl.ANY),
                pl.BlockSpec((width, width_out), lambda i, *_: (0, 0)),
                pl.BlockSpec((group, per_block, blk, blk), lambda i, *_: (work(i), 0, 0, 0)),
                pl.BlockSpec((sections, group * blk, blk), lambda i, *_: (0, work(i), 0)),
                pl.BlockSpec((group * blk, width_out), lambda i, *_: (work(i), 0)),
            ],
            out_specs=[
                pl.BlockSpec((group * blk, width_out), lambda i, *_: (work(i), 0)),
                pl.BlockSpec((peers // finals, height1, width), lambda i, *_: (final(i), 0, 0)),
                pl.BlockSpec((group * blk, width), lambda i, *_: (work(i), 0)),
            ],
            scratch_shapes=[
                pltpu.VMEM((blocks + peers, blk, width), BF),
                pltpu.VMEM((sections, peers, width), F32),
                pltpu.VMEM((sections * blk, width), BF),
                pltpu.VMEM((blocks + peers, KEPT, width), F32),
                pltpu.VMEM((width, sections * blk), F32),
                pltpu.VMEM((width, width_out), F32),
                pltpu.VMEM((peers, EXTRA, width), F32),
                pltpu.SemaphoreType.DMA((2,)),
            ],
        ),
        out_shape=[
            jax.ShapeDtypeStruct((rows, width_out), BF),
            jax.ShapeDtypeStruct((peers, height1, width), BF),
            jax.ShapeDtypeStruct((rows, width), BF),
        ],
        compiler_params=pltpu.CompilerParams(vmem_limit_bytes=LAYER_LIMIT),
    )(
        tile_columns.reshape(-1),
        features.reshape(blocks, blk, width),
        halo1.reshape(-1, width),
        halo2,
        weight,
        tiles,
        hub_tiles,
        cotangent,
    )


def rest_kernel(group, steps, columns_ref, back_ref, tiles_ref, send_ref, own_ref, adjoint):
    step = pl.program_id(0)
    per_block, blk = tiles_ref.shape[1:3]
    width = back_ref.shape[1]
    own_part = own_ref.shape[0] // blk
    send_part, height, _ = send_ref.shape
    own_blocks = own_part * (pl.num_programs(0) - steps)

    @pl.when(step == 0)
    def _():
        def clear(block, carry):
            adjoint[block] = jnp.zeros((blk, width), F32)
            return carry

        lax.fori_loop(0, adjoint.shape[0], clear, 0, unroll=4)

    @pl.when(step < steps)
    def _():
        for u in range(group):
            first = (step * group + u) * per_block
            slab = jnp.concatenate([tiles_ref[u, t] for t in range(per_block)], axis=1)
            spread = lax.dot_general(
                slab,
                back_ref[u * blk : (u + 1) * blk, :],
                (((0,), (0,)), ((), ())),
                preferred_element_type=F32,
            )
            for t in range(per_block):
                adjoint[columns_ref[first + t]] += spread[t * blk : (t + 1) * blk]

    @pl.when(step >= steps)
    def _():
        final = step - steps
        for block in range(own_part):
            own_ref[pl.ds(block * blk, blk), :] = adjoint[final * own_part + block]

        def finish(k, carry):
            rows = adjoint[own_blocks + final * send_part + k]
            tail = jnp.zeros((EXTRA, width), F32)
            send_ref[k] = jnp.concatenate([rows[blk + EXTRA - height :], tail], axis=0).astype(BF)
            return carry

        lax.fori_loop(0, send_part, finish, 0, unroll=4)


def rest_of_adjoint(back, tiles, tile_columns, peers):
    blocks, per_block, blk, _ = tiles.shape
    rows, width = back.shape
    group = 8
    steps = blocks // group
    finals = 4
    height = blk - FIRST_BACK + EXTRA

    def work(i):
        return jnp.minimum(i, steps - 1)

    def final(i):
        return jnp.maximum(i - steps, 0)

    return pl.pallas_call(
        functools.partial(rest_kernel, group, steps),
        grid_spec=pltpu.PrefetchScalarGridSpec(
            num_scalar_prefetch=1,
            grid=(steps + finals,),
            in_specs=[
                pl.BlockSpec((group * blk, width), lambda i, *_: (work(i), 0)),
                pl.BlockSpec((group, per_block, blk, blk), lambda i, *_: (work(i), 0, 0, 0)),
            ],
            out_specs=[
                pl.BlockSpec((peers // finals, height, width), lambda i, *_: (final(i), 0, 0)),
                pl.BlockSpec((rows // finals, width), lambda i, *_: (final(i), 0)),
            ],
            scratch_shapes=[pltpu.VMEM((blocks + peers, blk, width), F32)],
        ),
        out_shape=[
            jax.ShapeDtypeStruct((peers, height, width), BF),
            jax.ShapeDtypeStruct((rows, width), F32),
        ],
        compiler_params=pltpu.CompilerParams(vmem_limit_bytes=VMEM_LIMIT),
    )(tile_columns.reshape(-1), back, tiles)


def add_rows(totals, places, buffer, base):
    sums = [
        totals[v][pl.ds(place + PAD, 1), :] + buffer[pl.ds(base + v, 1), :]
        for v, place in enumerate(places)
    ]
    for v, place in enumerate(places):
        totals[v][pl.ds(place + PAD, 1), :] = sums[v]


def begin_totals(totals, start_ref):
    totals[0][pl.ds(PAD, start_ref.shape[0]), :] = start_ref[...]
    for total in totals[1:]:
        total[...] = jnp.zeros_like(total)


def sum_totals(totals, rows):
    live = pl.ds(PAD, rows)
    t0, t1, t2, t3 = totals
    return (t0[live, :] + t1[live, :]) + (t2[live, :] + t3[live, :])


def scatter_kernel(lists, slots, stop, list_ref, back_ref, start_ref, out_ref, t0, t1, t2, t3, buffer):
    step = pl.program_id(0)
    totals = (t0, t1, t2, t3)
    group = 16

    @pl.when(step == 0)
    def _():
        begin_totals(totals, start_ref)

    def one_list(k, carry):
        start = (step * lists + k) * slots
        buffer[...] = back_ref[k].astype(F32)

        def work(base, end):
            for slot in range(base, end, 4):
                places = [list_ref[start + slot + v] for v in range(4)]
                add_rows(totals, places, buffer, slot)

        work(0, LIVE)
        each_live_group(list_ref, start, LIVE, stop, group, work)
        return carry

    lax.fori_loop(0, lists, one_list, 0)

    @pl.when(step == pl.num_programs(0) - 1)
    def _():
        out_ref[...] = sum_totals(totals, start_ref.shape[0])


def scatter_first(send_lists, returned, start):
    peers, slots = send_lists.shape
    rows, width = start.shape
    lists = 32
    height = returned.shape[1]
    return pl.pallas_call(
        functools.partial(scatter_kernel, lists, slots, height - EXTRA),
        grid_spec=pltpu.PrefetchScalarGridSpec(
            num_scalar_prefetch=1,
            grid=(peers // lists,),
            in_specs=[
                pl.BlockSpec((lists, height, width), lambda i, *_: (i, 0, 0)),
                pl.BlockSpec((rows, width), lambda i, *_: (0, 0)),
            ],
            out_specs=pl.BlockSpec((rows, width), lambda i, *_: (0, 0)),
            scratch_shapes=[pltpu.VMEM((rows + PAD, width), F32)] * 4
            + [pltpu.VMEM((height, width), F32)],
        ),
        out_shape=jax.ShapeDtypeStruct((rows, width), F32),
        compiler_params=pltpu.CompilerParams(vmem_limit_bytes=VMEM_LIMIT),
    )(send_lists.reshape(-1), returned, start)


def last_kernel(
    sections,
    list_ref,
    hub_ref,
    owned_ref,
    back_ref,
    start_ref,
    out_ref,
    grad_w_ref,
    t0,
    t1,
    t2,
    t3,
    buffer,
    grad_w,
):
    totals = (t0, t1, t2, t3)
    peers, height, width = back_ref.shape
    count = height - EXTRA
    group = 16
    pieces = grad_w_ref.shape[1] // width
    begin_totals(totals, start_ref)

    def widen(part, carry):
        for k in range(8):
            peer = part * 8 + k
            buffer[peer] = back_ref[peer].astype(F32)
            for piece in range(pieces):
                high = count + sections + piece
                low = high + pieces
                grad_w[piece, pl.ds(peer, 1), :] = (
                    buffer[peer, high : high + 1, :] + buffer[peer, low : low + 1, :]
                )
        return carry

    lax.fori_loop(0, peers // 8, widen, 0)

    def one_list(peer, carry):
        rows = buffer.at[peer]

        def work(base, end):
            for slot in range(base, end, 4):
                places = [list_ref[peer * count + slot + v] for v in range(4)]
                add_rows(totals, places, rows, slot)

        each_live_group(list_ref, peer * count, 0, count, group, work)
        return carry

    lax.fori_loop(0, peers, one_list, 0, unroll=2)

    for section in range(sections):

        @pl.when(owned_ref[section] != 0)
        def _():
            def some_rows(part, carry):
                for k in range(0, group, 4):
                    for v in range(4):
                        peer = part * group + k + v
                        place = hub_ref[section * peers + peer] + PAD
                        row = buffer[peer, count + section : count + section + 1, :]
                        totals[v][pl.ds(place, 1), :] += row
                return carry

            lax.fori_loop(0, peers // group, some_rows, 0)

    for piece in range(pieces):
        grad_w_ref[:, piece * width : (piece + 1) * width] = grad_w[piece]
    out_ref[...] = sum_totals(totals, start_ref.shape[0]).astype(BF)


def scatter_last(send_lists, hub_rows, owned, returned, start, width_out):
    peers = send_lists.shape[0]
    rows, width = start.shape
    height = returned.shape[1]
    return pl.pallas_call(
        functools.partial(last_kernel, hub_rows.shape[0]),
        grid_spec=pltpu.PrefetchScalarGridSpec(
            num_scalar_prefetch=3,
            grid=(1,),
            in_specs=[
                pl.BlockSpec((peers, height, width), lambda i, *_: (0, 0, 0)),
                pl.BlockSpec((rows, width), lambda i, *_: (0, 0)),
            ],
            out_specs=[
                pl.BlockSpec((rows, width), lambda i, *_: (0, 0)),
                pl.BlockSpec((width, width_out), lambda i, *_: (0, 0)),
            ],
            scratch_shapes=[pltpu.VMEM((rows + PAD, width), F32)] * 4
            + [
                pltpu.VMEM((peers, height, width), F32),
                pltpu.VMEM((width_out // width, peers, width), F32),
            ],
        ),
        out_shape=[
            jax.ShapeDtypeStruct((rows, width), BF),
            jax.ShapeDtypeStruct((width, width_out), F32),
        ],
        compiler_params=pltpu.CompilerParams(vmem_limit_bytes=VMEM_LIMIT),
    )(send_lists.reshape(-1), hub_rows.reshape(-1), owned, returned, start)


def exchange(array):
    return lax.all_to_all(array, "rows", split_axis=0, concat_axis=0, tiled=True)


def body(
    features,
    weight,
    adjacency_tiles,
    tile_columns,
    send_rows,
    hub_owner,
    hub_rows,
    hub_tiles,
    cotangent,
):
    device = lax.axis_index("rows")
    sections, peers = hub_rows.shape
    width, width_out = weight.shape
    pieces = width_out // width
    send_lists = send_rows[0]
    slots = send_lists.shape[1]

    halo1 = exchange(gather_rows(features, send_lists, hub_rows, 0, FIRST_OUT))
    part = gather_rows(features, send_lists, hub_rows, FIRST_OUT, slots)
    hub_mine = halo1[hub_owner, FIRST_OUT + jnp.arange(sections)]
    part = part.at[:, :sections].set(
        jnp.broadcast_to(hub_mine[None], (peers, sections, width))
    )
    halo2 = exchange(part)

    output, send1, back = layer(
        features, halo1, halo2, weight, adjacency_tiles, tile_columns, hub_tiles, cotangent
    )

    back1 = exchange(send1)
    send2, own = rest_of_adjoint(back, adjacency_tiles, tile_columns, peers)
    sums = jnp.sum(back1[:, FIRST_BACK:].astype(F32), axis=0)
    weight_row = sums[sections : sections + pieces] + sums[sections + pieces :]
    high = weight_row.astype(BF)
    low = (weight_row - high.astype(F32)).astype(BF)
    mine = jnp.concatenate([sums[:sections].astype(BF), high, low], axis=0)
    end = slots - FIRST_BACK
    send2 = send2.at[:, end:].set(jnp.broadcast_to(mine[None], (peers,) + mine.shape))
    back2 = exchange(send2)

    owned = (hub_owner == device).astype(jnp.int32)
    total = scatter_first(send_lists, back1, own)
    grad_features, grad_weight = scatter_last(
        send_lists[:, FIRST_BACK:], hub_rows, owned, back2, total, width_out
    )
    return (output, grad_features, grad_weight)


def solution(mesh):
    return jax.shard_map(
        body,
        mesh=mesh,
        in_specs=(
            P("rows", None),
            P(),
            P("rows", None, None, None),
            P("rows", None),
            P("rows", None, None),
            P(),
            P(),
            P(None, "rows", None),
            P("rows", None),
        ),
        out_specs=(P("rows", None), P("rows", None), P()),
        check_vma=False,
    )
```
